32 devices in a mesh: shard: 4 (over z), tensor: 4 (over y, core), section: 2 (over x).
Axes of the slice: x: 2, y: 2, z: 4, core: 2. Of those that a mesh axis runs over, the one named last changes fastest.
Arguments:
- grads: bfloat16 [4, 4, 3072, 768], P('shard', 'section', 'tensor'), may hold values from -120 to 120
- weights: bfloat16 [4, 3072, 768], P('section', 'tensor'), may hold values from -3 to 3
- basis: float32 [4, 768, 256], P('section'), may hold values from -6 to 6
- first_moment: float32 [4, 3072, 256], P('section', ('tensor', 'shard')), may hold values from -6 to 6
- second_moment: float32 [4, 3072, 256], P('section', ('tensor', 'shard')), may hold values from 0.1 to 4
Outputs:
- weights_next: bfloat16 [4, 3072, 768], P('section', 'tensor')
- basis_next: float32 [4, 768, 256], P('section')
- moment_one: float32 [4, 3072, 256], P('section', ('tensor', 'shard'))
- moment_two: float32 [4, 3072, 256], P('section', ('tensor', 'shard'))
The draws below stay inside these ranges and needn't reach their ends.
All inputs are finite; a program needn't handle non-finite values.
Results may differ from the reference program's by a relative error of at most 0.0004.
Values may be sent and summed in bfloat16 or wider, within the bound.
No kernel may reach another device: no remote copies, remote signals or barrier semaphores. Data moves between devices by JAX's collectives and lax.ppermute only.
A program may use at most 64 MiB of HBM per device.

```python
import math
import jax
import jax.numpy as jnp
from jax import lax

D = 768
FF = 3072
RANK = 256
NS_ITERS = 3
STEP = 1000
LAYERS = 4
SHARDS = 4
ROWS_DEV = 192


def draw_grads(key, part):
    subkeys = jax.random.split(jax.random.fold_in(key, 17), 4)
    full_shape = (SHARDS, LAYERS, FF, D)
    base_draw = jnp.clip(jax.random.normal(subkeys[0], full_shape, jnp.float32), -6.0, 6.0)
    row_scale = jnp.exp(jax.random.uniform(subkeys[1], (1, LAYERS, FF, 1), jnp.float32) * math.log(10.0))
    column_scale = jnp.exp(jax.random.uniform(subkeys[3], (1, LAYERS, 1, D), jnp.float32) * math.log(10.0))
    pairing = jax.random.permutation(subkeys[2], SHARDS)
    blocks = jnp.arange(FF) // ROWS_DEV % SHARDS
    spike_gain = jnp.where(blocks[None, :] == pairing[:, None], 4.0, 1.0)
    values = 0.05 * base_draw * row_scale * column_scale * spike_gain[:, None, :, None]
    return values.astype(jnp.bfloat16)


def block_levels(rng, dims, pieces, smallest, top_value):
    factor_of = 1.0
    for position, blocks in pieces:
        steps = jax.random.uniform(jax.random.fold_in(jax.random.fold_in(rng, 6), position), (blocks,), jnp.float32, smallest / len(pieces), top_value / len(pieces))
        factor_of = factor_of * jnp.repeat(jnp.exp(steps), dims[position] // blocks).reshape((-1,) + (1,) * (len(dims) - 1 - position))
    return factor_of


def bell_draw(rng, extent, deviation, most, shards=(), held_as=jnp.bfloat16):
    gain = block_levels(rng, extent, shards, -0.22, 0.18) if shards else 1.0
    drawn = jax.random.normal(rng, extent, jnp.float32) * deviation * gain
    return jnp.minimum(jnp.maximum(drawn, -most), most).astype(held_as)


def setup_inputs(seed: int = 0) -> dict:
    splits = jax.random.split(jax.random.key(seed), 6)
    return {
        "grads": draw_grads(jax.random.fold_in(splits[5], 71), 0),
        "weights": bell_draw(splits[1], (LAYERS, FF, D), 0.5, 3.0, ((0, 2), (1, 4))),
        "basis": bell_draw(splits[2], (LAYERS, D, RANK), 1.0, 6.0, ((0, 2),), jnp.float32),
        "first_moment": bell_draw(splits[3], (LAYERS, FF, RANK), 1.0, 6.0, ((0, 2), (1, 16)), jnp.float32),
        "second_moment": jnp.clip(jnp.exp(math.log(4.0) - 3.6888794 * jax.random.uniform(splits[4], (LAYERS, FF, RANK), jnp.float32) ** block_levels(splits[4], (LAYERS, FF, RANK), ((0, 2), (1, 16)), -0.2, 0.2)), 0.1, 4.0),
    }


learn_rate = 0.5
galore_scale = 0.25
beta_one = 0.9
beta_two = 0.999
adam_eps = 1e-08
norm_eps = 1e-07
coeff_a = 3.4445
coeff_b = -4.775
coeff_c = 2.0315
highest = lax.Precision.HIGHEST

def newton_step(iterate, gram_matrix):
    squared = jnp.einsum('lrs,lst->lrt', gram_matrix, gram_matrix, precision=highest)
    mixing = coeff_b * gram_matrix + coeff_c * squared
    return coeff_a * iterate + jnp.einsum('ldr,lrs->lds', iterate, mixing, precision=highest)

def adam_direction(reduced, first_moment, second_moment):
    moment_one = beta_one * first_moment + (1.0 - beta_one) * reduced
    moment_two = beta_two * second_moment + (1.0 - beta_two) * reduced * reduced
    corrected_one = moment_one / (1.0 - beta_one ** STEP)
    corrected_two = moment_two / (1.0 - beta_two ** STEP)
    return (moment_one, moment_two, corrected_one / (jnp.sqrt(corrected_two) + adam_eps))

def reference(grads, weights, basis, first_moment, second_moment):

    def accumulate(running, block_grad):
        return (running + block_grad.astype(jnp.float32), None)
    summed, leftover = lax.scan(accumulate, jnp.zeros(weights.shape, jnp.float32), grads)
    scale_factor = D ** (-0.5)
    projected = jnp.einsum('lfd,ldr->lfr', summed, basis, precision=highest)
    reduced = scale_factor * projected
    moment_one, moment_two, direction = adam_direction(reduced, first_moment, second_moment)
    update = jnp.einsum('lfr,ldr->lfd', direction, basis, precision=highest)
    factor = learn_rate * galore_scale * scale_factor
    weights_next = (weights.astype(jnp.float32) - factor * update).astype(jnp.bfloat16)
    power = jnp.einsum('lfd,lfr->ldr', summed, projected, precision=highest)
    norms = jnp.sqrt(lax.optimization_barrier(jnp.sum(power * power, axis=(1, 2))))
    iterate = power / (norms + norm_eps)[:, None, None]
    for sweep in range(NS_ITERS):
        gram_matrix = jnp.einsum('ldr,lds->lrs', iterate, iterate, precision=highest)
        iterate = newton_step(iterate, gram_matrix)
    basis_next = D ** 0.5 * iterate
    return (weights_next, basis_next, moment_one, moment_two)
```

```python
import jax
import jax.numpy as jnp
from jax import lax
from jax.sharding import PartitionSpec as P

NS_ITERS = 3
STEP = 1000


learn_rate = 0.5
galore_scale = 0.25
beta_one = 0.9
beta_two = 0.999
adam_eps = 1e-08
norm_eps = 1e-07
coeff_a = 3.4445
coeff_b = -4.775
coeff_c = 2.0315
highest = lax.Precision.HIGHEST


def newton_step(iterate, gram_matrix):
    squared = jnp.einsum("lrs,lst->lrt", gram_matrix, gram_matrix, precision=highest)
    mixing = coeff_b * gram_matrix + coeff_c * squared
    return coeff_a * iterate + jnp.einsum("ldr,lrs->lds", iterate, mixing, precision=highest)


def adam_direction(reduced, first_moment, second_moment):
    moment_one = beta_one * first_moment + (1.0 - beta_one) * reduced
    moment_two = beta_two * second_moment + (1.0 - beta_two) * reduced * reduced
    corrected_one = moment_one / (1.0 - beta_one**STEP)
    corrected_two = moment_two / (1.0 - beta_two**STEP)
    return (moment_one, moment_two, corrected_one / (jnp.sqrt(corrected_two) + adam_eps))


def newton_schulz(power, width):
    norms = jnp.sqrt(jnp.sum(power * power, axis=(1, 2)))
    iterate = power / (norms + norm_eps)[:, None, None]
    for sweep in range(NS_ITERS):
        gram_matrix = jnp.einsum("ldr,lds->lrs", iterate, iterate, precision=highest)
        iterate = newton_step(iterate, gram_matrix)
    return width**0.5 * iterate


def general_body(grads, weights, basis, first_moment, second_moment):
    width = basis.shape[1]
    scale_factor = width ** (-0.5)
    local_grads = grads[0]
    block_rows = first_moment.shape[1]
    summed = lax.psum_scatter(
        local_grads.astype(jnp.float32), "shard", scatter_dimension=1, tiled=True
    )
    projected = jnp.einsum("lfd,ldr->lfr", summed, basis, precision=highest)
    power = jnp.einsum("lfd,lfr->ldr", summed, projected, precision=highest)
    reduced = scale_factor * projected
    moment_one, moment_two, direction = adam_direction(reduced, first_moment, second_moment)
    factor = learn_rate * galore_scale * scale_factor
    own_start = lax.axis_index("shard") * block_rows
    current = lax.dynamic_slice_in_dim(weights, own_start, block_rows, 1)
    update = jnp.einsum("lfr,ldr->lfd", direction, basis, precision=highest)
    fresh_rows = (current.astype(jnp.float32) - factor * update).astype(jnp.bfloat16)
    weights_next = lax.all_gather(fresh_rows, "shard", axis=1, tiled=True)
    whole = lax.psum(power, ("shard", "tensor"))
    basis_next = newton_schulz(whole, width)
    return (weights_next, basis_next, moment_one, moment_two)


def xor_pairs(k):
    return [(i, i ^ k) for i in range(4)]


def over_z(x, k):
    return lax.ppermute(x, "shard", xor_pairs(k))


def over_core(x):
    return lax.ppermute(x, "tensor", xor_pairs(1))


def over_y(x):
    return lax.ppermute(x, "tensor", xor_pairs(2))


def halves(x, low_first):
    rows = x.shape[0] // 2
    keep = lax.dynamic_slice_in_dim(x, low_first * rows, rows, 0)
    give = lax.dynamic_slice_in_dim(x, (1 - low_first) * rows, rows, 0)
    return keep, give


def join(own, other, place):
    return jnp.where(place == 0, jnp.concatenate([own, other]), jnp.concatenate([other, own]))


def sum_power(power, z, y, core):
    keep, give = halves(power, core)
    power = keep + over_core(give)
    keep, give = halves(power, y)
    power = keep + over_y(give)
    rows = power.shape[0] // 4
    part = lambda b: lax.dynamic_slice_in_dim(power, b * rows, rows, 0)
    mine = part(z) + over_z(part(z ^ 3), 3) + over_z(part(z ^ 2), 2) + over_z(part(z ^ 1), 1)
    whole = jnp.zeros_like(power)
    for k, block in ((0, mine), (1, over_z(mine, 1)), (2, over_z(mine, 2)), (3, over_z(mine, 3))):
        whole = lax.dynamic_update_slice_in_dim(whole, block, (z ^ k) * rows, 0)
    whole = join(whole, over_y(whole), y)
    return join(whole, over_core(whole), core)


def line_body(grads, weights, basis, first_moment, second_moment):
    width = basis.shape[1]
    scale_factor = width ** (-0.5)
    layers = grads.shape[1]
    rows = first_moment.shape[1]
    z = lax.axis_index("shard")
    tensor = lax.axis_index("tensor")
    y, core = tensor // 2, tensor % 2
    outer = (z == 0) | (z == 3)

    def block(layer, index):
        return lax.dynamic_slice_in_dim(grads[0, layer], index * rows, rows, 0)

    summed = []
    for layer in range(layers):
        for j in range(2):
            keep = block(layer, jnp.where(outer, 3 * j, 1 + j))
            give = block(layer, jnp.where(outer, 1 + j, 3 * j))
            summed.append(keep.astype(jnp.float32) + over_z(give, 1).astype(jnp.float32))
    projected = []
    for index, half_sum in enumerate(summed):
        partial = jnp.einsum("fd,dr->fr", half_sum, basis[index // 2], precision=highest)
        projected.append(partial + over_z(partial, 3))

    powers = []
    for layer in range(layers):
        own = sum(
            jnp.einsum("fd,fr->dr", summed[2 * layer + j], projected[2 * layer + j], precision=highest)
            for j in range(2)
        )
        powers.append(sum_power(own, z, y, core))

    mine = jnp.stack([jnp.where(z < 2, projected[2 * l], projected[2 * l + 1]) for l in range(layers)])
    reduced = scale_factor * mine
    moment_one, moment_two, direction = adam_direction(reduced, first_moment, second_moment)
    factor = learn_rate * galore_scale * scale_factor
    far = over_z(direction, 3)
    parts = ((0, direction), (1, over_z(direction, 1)), (3, far), (2, over_z(far, 1)))
    directions = jnp.zeros((layers, 4 * rows, direction.shape[2]), jnp.float32)
    for k, part in parts:
        directions = lax.dynamic_update_slice_in_dim(directions, part, (z ^ k) * rows, 1)
    update = jnp.einsum("lfr,ldr->lfd", directions, basis, precision=highest)
    weights_next = (weights.astype(jnp.float32) - factor * update).astype(jnp.bfloat16)

    basis_next = jnp.concatenate([newton_schulz(power[None], width) for power in powers])
    return (weights_next, basis_next, moment_one, moment_two)


def solution(mesh):
    line = mesh.shape["shard"] == 4 and mesh.shape["tensor"] == 4
    return jax.shard_map(
        line_body if line else general_body,
        mesh=mesh,
        in_specs=(
            P("shard", "section", "tensor", None),
            P("section", "tensor", None),
            P("section", None, None),
            P("section", ("tensor", "shard"), None),
            P("section", ("tensor", "shard"), None),
        ),
        out_specs=(
            P("section", "tensor", None),
            P("section", None, None),
            P("section", ("tensor", "shard"), None),
            P("section", ("tensor", "shard"), None),
        ),
        check_vma=False,
    )
```

```python
import functools

import jax
import jax.numpy as jnp
from jax import lax
from jax.experimental import pallas as pl
from jax.experimental.pallas import tpu as pltpu
from jax.sharding import PartitionSpec as P

NS_ITERS = 3
STEP = 1000


learn_rate = 0.5
galore_scale = 0.25
beta_one = 0.9
beta_two = 0.999
adam_eps = 1e-08
norm_eps = 1e-07
coeff_a = 3.4445
coeff_b = -4.775
coeff_c = 2.0315
highest = lax.Precision.HIGHEST


def newton_step(iterate, gram_matrix):
    squared = jnp.einsum("lrs,lst->lrt", gram_matrix, gram_matrix, precision=highest)
    mixing = coeff_b * gram_matrix + coeff_c * squared
    return coeff_a * iterate + jnp.einsum("ldr,lrs->lds", iterate, mixing, precision=highest)


def adam_direction(reduced, first_moment, second_moment):
    moment_one = beta_one * first_moment + (1.0 - beta_one) * reduced
    moment_two = beta_two * second_moment + (1.0 - beta_two) * reduced * reduced
    corrected_one = moment_one / (1.0 - beta_one**STEP)
    corrected_two = moment_two / (1.0 - beta_two**STEP)
    return (moment_one, moment_two, corrected_one / (jnp.sqrt(corrected_two) + adam_eps))


def newton_schulz(power, width):
    norms = jnp.sqrt(jnp.sum(power * power, axis=(1, 2)))
    iterate = power / (norms + norm_eps)[:, None, None]
    for sweep in range(NS_ITERS):
        gram_matrix = jnp.einsum("ldr,lds->lrs", iterate, iterate, precision=highest)
        iterate = newton_step(iterate, gram_matrix)
    return width**0.5 * iterate


def general_body(grads, weights, basis, first_moment, second_moment):
    width = basis.shape[1]
    scale_factor = width ** (-0.5)
    local_grads = grads[0]
    block_rows = first_moment.shape[1]
    summed = lax.psum_scatter(
        local_grads.astype(jnp.float32), "shard", scatter_dimension=1, tiled=True
    )
    projected = jnp.einsum("lfd,ldr->lfr", summed, basis, precision=highest)
    power = jnp.einsum("lfd,lfr->ldr", summed, projected, precision=highest)
    reduced = scale_factor * projected
    moment_one, moment_two, direction = adam_direction(reduced, first_moment, second_moment)
    factor = learn_rate * galore_scale * scale_factor
    own_start = lax.axis_index("shard") * block_rows
    current = lax.dynamic_slice_in_dim(weights, own_start, block_rows, 1)
    update = jnp.einsum("lfr,ldr->lfd", direction, basis, precision=highest)
    fresh_rows = (current.astype(jnp.float32) - factor * update).astype(jnp.bfloat16)
    weights_next = lax.all_gather(fresh_rows, "shard", axis=1, tiled=True)
    whole = lax.psum(power, ("shard", "tensor"))
    basis_next = newton_schulz(whole, width)
    return (weights_next, basis_next, moment_one, moment_two)


PLAIN = ((1,), (0,))
BOTH_LAST = ((1,), (1,))
CORE, Z, Y = 2, 3, 4


def split(x):
    high = x.astype(jnp.bfloat16)
    return high, (x - high.astype(jnp.float32)).astype(jnp.bfloat16)


def dot3(a, b, dims=PLAIN):
    dot = lambda p, q: lax.dot_general(p, q, (dims, ((), ())), preferred_element_type=jnp.float32)
    return dot(a[0], b[0]) + (dot(a[0], b[1]) + dot(a[1], b[0]))


def params(megabytes):
    return pltpu.CompilerParams(vmem_limit_bytes=megabytes * 2**20)


def in_vmem(*arrays):
    return [pltpu.with_memory_space_constraint(x, pltpu.VMEM) for x in arrays]


def local_call(kernel, outs, index, *operands, name, scratch=()):
    vmem = pl.BlockSpec(memory_space=pltpu.VMEM)
    return pl.pallas_call(
        kernel,
        out_shape=[(jax.ShapeDtypeStruct if name == "moments" and i < 2 else pltpu.VMEM)(*out) for i, out in enumerate(outs)],
        in_specs=[pl.BlockSpec(memory_space=pltpu.SMEM)] + [vmem] * len(operands),
        out_specs=[vmem] * len(outs),
        scratch_shapes=scratch,
        compiler_params=params(12),
        name=name,
    )(index, *in_vmem(*operands))


def chunks(rows):
    half = rows // 2
    return ((0, 0, 0, rows), (0, 1, 0, rows), (1, 0, 0, rows), (1, 1, 0, half), (1, 1, half, half))


def layer_of(index_ref, turn):
    return index_ref[CORE] if turn else 1 - index_ref[CORE]


def give_kernel(rows, grads_ref, *rest):
    outs, sems = rest[:-1], rest[-1]
    outer = lax.rem(lax.axis_index("shard") + 1, 4) <= 1
    core = lax.rem(lax.axis_index("tensor"), 2)
    copies = []
    for i, out in enumerate(outs):
        block = jnp.where(outer, 1 + i % 2, 3 * (i % 2))
        start = pl.multiple_of(block * rows, rows)
        layer = 1 - core if i < 2 else core
        copies.append(pltpu.make_async_copy(grads_ref.at[0, layer, pl.ds(start, rows)], out, sems.at[i]))
    for copy in copies:
        copy.start()
    for copy in copies:
        copy.wait()


def give_blocks(grads, rows):
    count = 4
    return pl.pallas_call(
        functools.partial(give_kernel, rows),
        out_shape=[pltpu.VMEM((rows, grads.shape[3]), grads.dtype)] * count,
        in_specs=[pl.BlockSpec(memory_space=pltpu.HBM)],
        out_specs=[pl.BlockSpec(memory_space=pltpu.VMEM)] * count,
        scratch_shapes=[pltpu.SemaphoreType.DMA((count,))],
        compiler_params=params(4),
        name="give_blocks",
    )(pltpu.with_memory_space_constraint(grads, pltpu.HBM))


def kept_sum(index_ref, grads_ref, other_ref, chunk, rows):
    turn, j, row, count = chunk
    start = pl.multiple_of(index_ref[j] * rows + row, count)
    kept = grads_ref[0, layer_of(index_ref, turn), pl.ds(start, count)]
    return kept.astype(jnp.float32) + other_ref[pl.ds(row, count)].astype(jnp.float32)


def project_kernel(chunk, rows, index_ref, grads_ref, other_ref, basis_ref, *refs):
    total = kept_sum(index_ref, grads_ref, other_ref, chunk, rows)
    projected = dot3(split(total), split(basis_ref[layer_of(index_ref, chunk[0])]))
    if len(refs) == 1:
        refs[0][...] = projected
        return
    *before, out_ref, far0_ref, far1_ref = refs
    out_ref[...] = projected
    for (turn, j, row, count), part in zip(chunks(rows), before):
        (far0_ref, far1_ref)[turn][pl.ds(j * rows + row, count)] = part[...]
    far1_ref[pl.ds(2 * rows - projected.shape[0], projected.shape[0])] = projected


def project(index, grads, other, basis, chunk, rows, before=()):
    rank = basis.shape[2]
    kernel = functools.partial(project_kernel, chunk, rows)
    outs = [((chunk[3], rank), jnp.float32)] + [((2 * rows, rank), jnp.float32)] * (2 if before else 0)
    return local_call(kernel, outs, index, grads, other, basis, *before, name="project")


HALVES = 2


def place_of(index_ref, h, k, piece):
    place = h * 4 + (index_ref[Y] ^ (k // 2)) * 2 + (index_ref[0] ^ (k % 2))
    return pl.multiple_of(place * piece, piece)


def power_kernel(turn, rows, index_ref, grads_ref, *refs):
    mine_chunks = [chunk for chunk in chunks(rows) if chunk[0] == turn]
    n = len(mine_chunks)
    others, partials, inner, (far_ref, *rest) = refs[:n], refs[n : 2 * n], refs[2 * n : 3 * n], refs[3 * n :]
    sums, summed = [], []
    for chunk, other, partial, received in zip(mine_chunks, others, partials, inner):
        _, j, row, count = chunk
        summed.append(kept_sum(index_ref, grads_ref, other, chunk, rows))
        sums.append(partial[...] + (received[...] + far_ref[pl.ds(j * rows + row, count)]))
    projected, summed = jnp.concatenate(sums), jnp.concatenate(summed)
    total = dot3(split(projected.T), split(summed))
    *halves, mine_ref, scratch = rest
    mine_ref[...] = jnp.where(index_ref[Z] < 2, projected[:rows], projected[rows:])
    scratch[...] = total
    piece = total.shape[0] // (4 * HALVES)
    for h in range(HALVES):
        for k in range(4):
            halves[h][pl.ds(k * piece, piece)] = scratch[pl.ds(place_of(index_ref, h, k, piece), piece)]


def power_product(index, grads, others, partials, inner, far, turn):
    width, rank, rows = grads.shape[3], far.shape[1], far.shape[0] // 2
    outs = [((rank // HALVES, width), jnp.float32)] * HALVES + [((rows, rank), jnp.float32)]
    kernel = functools.partial(power_kernel, turn, rows)
    scratch = [pltpu.VMEM((rank, width), jnp.float32)]
    return local_call(kernel, outs, index, grads, *others, *partials, *inner, far, name="power", scratch=scratch)


def add_split_kernel(index_ref, own_ref, received_ref, keep_ref, give_ref):
    half = keep_ref.shape[0]
    keep_ref[...] = own_ref[0:half] + received_ref[0:half]
    give_ref[...] = own_ref[half:] + received_ref[half:]


def add_split(index, own, received):
    outs = [((own.shape[0] // 2, own.shape[1]), jnp.float32)] * 2
    return local_call(add_split_kernel, outs, index, own, received, name="add_split")


def newton_schulz_kernel(index_ref, *refs):
    parts, (out_ref, result_ref, power_ref, sems) = refs[:-4], refs[-4:]
    piece = parts[0].shape[0] // 2
    for h in range(HALVES):
        for k in range(4):
            part = parts[2 * h + k // 2]
            power_ref[pl.ds(place_of(index_ref, h, k, piece), piece)] = part[pl.ds(k % 2 * piece, piece)]
    power = power_ref[...]
    rank, width = power.shape
    unscaled = split(power)
    scale = 1.0 / (jnp.sqrt(jnp.sum(power * power)) + norm_eps)
    gram = dot3(unscaled, unscaled, BOTH_LAST) * scale * scale
    ident = lax.broadcasted_iota(jnp.int32, gram.shape, 0) == lax.broadcasted_iota(jnp.int32, gram.shape, 1)
    diagonal = jnp.where(ident, coeff_a, 0.0)
    product = None
    for sweep in range(NS_ITERS - 1):
        g = split(gram)
        factor = diagonal + coeff_b * gram + coeff_c * dot3(g, g)
        f = split(factor)
        gram = dot3(split(dot3(f, g)), f)
        product = f if product is None else split(dot3(product, f))
    iterate = split(dot3(product, unscaled))
    g = split(gram)
    last = split((diagonal + coeff_b * gram + coeff_c * dot3(g, g)) * (scale * width**0.5))
    copies = []
    for i in range(width // rank):
        columns = slice(i * rank, (i + 1) * rank)
        result_ref[columns] = dot3(last, [term[:, columns] for term in iterate]).T
        copies.append(pltpu.make_async_copy(result_ref.at[columns], out_ref.at[index_ref[CORE], columns], sems.at[i]))
        copies[-1].start()
    for copy in copies:
        copy.wait()


def newton_schulz_power(index, layers, *parts):
    rank, width = 2 * HALVES * parts[0].shape[0], parts[0].shape[1]
    vmem = pl.BlockSpec(memory_space=pltpu.VMEM)
    return pl.pallas_call(
        newton_schulz_kernel,
        out_shape=[jax.ShapeDtypeStruct((layers, width, rank), jnp.float32), pltpu.VMEM((width, rank), jnp.float32)],
        in_specs=[pl.BlockSpec(memory_space=pltpu.SMEM)] + [vmem] * len(parts),
        out_specs=[pl.BlockSpec(memory_space=pl.ANY), vmem],
        scratch_shapes=[pltpu.VMEM((rank, width), jnp.float32), pltpu.SemaphoreType.DMA((width // rank,))],
        compiler_params=params(12),
        name="newton_schulz",
    )(index, *in_vmem(*parts))


def put_layer_kernel(index_ref, layer_ref, whole_ref, out_ref, sem):
    copy = pltpu.make_async_copy(layer_ref, out_ref.at[1 - index_ref[CORE]], sem)
    copy.start()
    copy.wait()


def put_layer(index, layer, whole):
    hbm = pl.BlockSpec(memory_space=pl.ANY)
    return pl.pallas_call(
        put_layer_kernel,
        out_shape=jax.ShapeDtypeStruct(whole.shape, whole.dtype),
        in_specs=[pl.BlockSpec(memory_space=pltpu.SMEM), pl.BlockSpec(memory_space=pltpu.VMEM), hbm],
        out_specs=hbm,
        scratch_shapes=[pltpu.SemaphoreType.DMA],
        input_output_aliases={2: 0},
        compiler_params=params(4),
        name="put_layer",
    )(index, *in_vmem(layer), whole)


SPAN = 250.0


def encode(x):
    bound = jnp.max(jnp.abs(x), axis=0, keepdims=True)
    bound = (bound * 1.01 + 1e-30).astype(jnp.bfloat16).astype(jnp.float32)
    size = jnp.exp2(jnp.abs(x) * (SPAN / bound) - SPAN / 2)
    code = jnp.where(x < 0, -size, size)
    return code.astype(jnp.bfloat16), jnp.broadcast_to(bound, (16, x.shape[1])).astype(jnp.bfloat16)


def decode(code, bound):
    code, bound = code.astype(jnp.float32), bound[0:1].astype(jnp.float32)
    size = (jnp.log2(jnp.abs(code)) + SPAN / 2) * (bound / SPAN)
    return jnp.where(code < 0, -size, size)


def moments_kernel(scale, index_ref, mine0_ref, mine1_ref, first_ref, second_ref, one_ref, two_ref, code_ref):
    rows = first_ref.shape[1]
    for turn, mine in enumerate((mine0_ref, mine1_ref)):
        layer = layer_of(index_ref, turn)
        reduced = scale * mine[...]
        one_ref[layer], two_ref[layer], direction = adam_direction(reduced, first_ref[layer], second_ref[layer])
        code_ref[layer, 0:rows], code_ref[layer, rows:] = encode(direction)


def moments(index, mine, first_moment, second_moment, scale):
    layers, rows, rank = first_moment.shape
    outs = [(first_moment.shape, jnp.float32)] * 2 + [((layers, rows + 16, rank), jnp.bfloat16)]
    return local_call(functools.partial(moments_kernel, scale), outs, index, *mine, first_moment, second_moment, name="moments")


def update_kernel(factor, index_ref, weights_ref, basis_ref, d0_ref, d1_ref, d2_ref, d3_ref, *rest):
    out_ref, high, low = rest[-3:]
    k = pl.program_id(0)

    @pl.when(k == 0)
    def _():
        high[...], low[...] = split(basis_ref[0].T)

    for step, direction in enumerate((d0_ref, d1_ref, d2_ref, d3_ref)):

        @pl.when(k == step)
        def _(direction=direction):
            rows = out_ref.shape[1]
            exact = decode(direction[0, 0:rows], direction[0, rows:])
            update = dot3(split(exact), (high[...], low[...]))
            out_ref[0] = (weights_ref[0].astype(jnp.float32) - factor * update).astype(out_ref.dtype)


def update_weights(index, weights, basis, directions, factor, layer, before):
    layers, height, width = weights.shape
    rank = basis.shape[2]
    rows = height // 4
    row_block = pl.BlockSpec((1, rows, width), lambda k, index: (layer, index[Z] ^ k, 0))
    layer_block = lambda a, b: pl.BlockSpec((1, a, b), lambda k, index: (layer, 0, 0))
    extra = [] if before is None else [before]
    return pl.pallas_call(
        functools.partial(update_kernel, factor),
        out_shape=jax.ShapeDtypeStruct(weights.shape, weights.dtype),
        grid_spec=pltpu.PrefetchScalarGridSpec(
            num_scalar_prefetch=1,
            grid=(4,),
            in_specs=[row_block, layer_block(width, rank)]
            + [layer_block(rows + 16, rank)] * 4
            + [pl.BlockSpec(memory_space=pl.ANY)] * len(extra),
            out_specs=row_block,
            scratch_shapes=[pltpu.VMEM((rank, width), jnp.bfloat16)] * 2,
        ),
        input_output_aliases={7: 0} if extra else {},
        compiler_params=params(12),
        name="update_weights",
    )(index, weights, basis, *directions, *extra)


def xor_pairs(k):
    return [(i, i ^ k) for i in range(4)]


OUTER, INNER = (0, 3), (1, 2)


def over_z(x, k, members=range(4)):
    return lax.ppermute(x, "shard", [pair for pair in xor_pairs(k) if pair[0] in members])


def over_core(x):
    return lax.ppermute(x, "tensor", xor_pairs(1))


def over_y(x):
    return lax.ppermute(x, "tensor", xor_pairs(2))


class Order:
    def __init__(self):
        self.last = None

    def step(self, *operands):
        if self.last is None:
            return operands
        return lax.optimization_barrier(tuple(operands) + (self.last,))[:-1]

    def through(self, result):
        self.last = result
        return result


def line_body(grads, weights, basis, first_moment, second_moment):
    width = basis.shape[1]
    scale_factor = width ** (-0.5)
    layers = grads.shape[1]
    rows = first_moment.shape[1]
    z = lax.axis_index("shard")
    tensor = lax.axis_index("tensor")
    y, core = tensor // 2, tensor % 2
    outer = (z == 0) | (z == 3)
    order = Order()

    keep = jnp.where(outer, jnp.array([0, 3], jnp.int32), jnp.array([1, 2], jnp.int32))
    index = jnp.concatenate([keep, jnp.stack([core, z, y]).astype(jnp.int32)])
    others = [over_z(block, 1) for block in give_blocks(grads, rows)]
    partials, inner = [], []
    for i, chunk in enumerate(chunks(rows)):
        other = others[2 * chunk[0] + chunk[1]]
        if i < 2:
            (other,) = order.step(other)
        else:
            other, inner[i - 2] = order.step(other, inner[i - 2])
        partial, *far = project(index, grads, other, basis, chunk, rows, partials if i == 4 else ())
        partials.append(order.through(partial))
        inner.append(over_z(partial, 3, INNER))
    *far, inner[3], inner[4] = order.step(*far, inner[3], inner[4])
    far = [over_z(part, 3, OUTER) for part in far]

    def product(turn):
        some = slice(0, 2) if turn == 0 else slice(2, 5)
        n = some.stop - some.start
        operands = order.step(*[others[2 * c[0] + c[1]] for c in chunks(rows)[some]], *partials[some], *inner[some], far[turn])
        *halves, mine = power_product(index, grads, operands[:n], operands[n : 2 * n], operands[2 * n : -1], operands[-1], turn)
        order.through(halves[0])
        return halves, mine

    def scatter(over, x, received):
        keep, give = add_split(index, *order.step(x, received))
        return order.through(keep), over(give)

    def total(over, x, received):
        x, received = order.step(x, received)
        x = order.through(x + received)
        return x, over(x)

    def gather(over, x, received):
        x = order.through(jnp.concatenate(order.step(x, received)))
        return x, over(x)

    next_z = lambda x: over_z(x, 1)
    opposite_z = lambda x: over_z(x, 3)

    gifts, mine0 = product(0)
    gifts = [over_core(gift) for gift in gifts]
    parts, mine1 = product(1)
    parts = [scatter(over_y, part, gift) for part, gift in zip(parts, gifts)]
    mine = order.step(mine0, mine1)
    moment_one, moment_two, code = moments(index, mine, first_moment, second_moment, scale_factor)
    order.through(code)
    opposite, near = opposite_z(code), next_z(code)
    parts = [scatter(next_z, *part) for part in parts]
    parts = [total(opposite_z, *part) for part in parts]
    opposite, near = order.step(opposite, near)
    next_to_opposite = next_z(opposite)
    parts = [total(next_z, *part) for part in parts]
    directions = (code, near, next_to_opposite, opposite)
    factor = learn_rate * galore_scale * scale_factor
    update = functools.partial(update_weights, index, weights, basis)
    weights_next = order.through(update(order.step(*directions), factor, 0, None))
    parts = [gather(over_y, *part) for part in parts]
    weights_next = order.through(update(order.step(*directions), factor, 1, weights_next))
    parts = order.step(*[x for part in parts for x in part])
    basis_next, own = newton_schulz_power(index, layers, *parts)
    basis_next = put_layer(index, over_core(own), basis_next)
    return (weights_next, basis_next, moment_one, moment_two)


def solution(mesh):
    line = mesh.shape["shard"] == 4 and mesh.shape["tensor"] == 4

    def body(grads, *others):
        return (line_body if line and grads.shape[1] == 2 else general_body)(grads, *others)

    return jax.shard_map(
        body,
        mesh=mesh,
        in_specs=(
            P("shard", "section", "tensor", None),
            P("section", "tensor", None),
            P("section", None, None),
            P("section", ("tensor", "shard"), None),
            P("section", ("tensor", "shard"), None),
        ),
        out_specs=(
            P("section", "tensor", None),
            P("section", None, None),
            P("section", ("tensor", "shard"), None),
            P("section", ("tensor", "shard"), None),
        ),
        check_vma=False,
    )
```

```python
import functools

import jax
import jax.numpy as jnp
from jax import lax
from jax.experimental import pallas as pl
from jax.experimental.pallas import tpu as pltpu
from jax.sharding import PartitionSpec as P

NS_ITERS = 3
STEP = 1000


learn_rate = 0.5
galore_scale = 0.25
beta_one = 0.9
beta_two = 0.999
adam_eps = 1e-08
norm_eps = 1e-07
coeff_a = 3.4445
coeff_b = -4.775
coeff_c = 2.0315
highest = lax.Precision.HIGHEST


def newton_step(iterate, gram_matrix):
    squared = jnp.einsum("lrs,lst->lrt", gram_matrix, gram_matrix, precision=highest)
    mixing = coeff_b * gram_matrix + coeff_c * squared
    return coeff_a * iterate + jnp.einsum("ldr,lrs->lds", iterate, mixing, precision=highest)


def adam_direction(reduced, first_moment, second_moment):
    moment_one = beta_one * first_moment + (1.0 - beta_one) * reduced
    moment_two = beta_two * second_moment + (1.0 - beta_two) * reduced * reduced
    corrected_one = moment_one / (1.0 - beta_one**STEP)
    corrected_two = moment_two / (1.0 - beta_two**STEP)
    return (moment_one, moment_two, corrected_one / (jnp.sqrt(corrected_two) + adam_eps))


def newton_schulz(power, width):
    norms = jnp.sqrt(jnp.sum(power * power, axis=(1, 2)))
    iterate = power / (norms + norm_eps)[:, None, None]
    for sweep in range(NS_ITERS):
        gram_matrix = jnp.einsum("ldr,lds->lrs", iterate, iterate, precision=highest)
        iterate = newton_step(iterate, gram_matrix)
    return width**0.5 * iterate


def general_body(grads, weights, basis, first_moment, second_moment):
    width = basis.shape[1]
    scale_factor = width ** (-0.5)
    local_grads = grads[0]
    block_rows = first_moment.shape[1]
    summed = lax.psum_scatter(
        local_grads.astype(jnp.float32), "shard", scatter_dimension=1, tiled=True
    )
    projected = jnp.einsum("lfd,ldr->lfr", summed, basis, precision=highest)
    power = jnp.einsum("lfd,lfr->ldr", summed, projected, precision=highest)
    reduced = scale_factor * projected
    moment_one, moment_two, direction = adam_direction(reduced, first_moment, second_moment)
    factor = learn_rate * galore_scale * scale_factor
    own_start = lax.axis_index("shard") * block_rows
    current = lax.dynamic_slice_in_dim(weights, own_start, block_rows, 1)
    update = jnp.einsum("lfr,ldr->lfd", direction, basis, precision=highest)
    fresh_rows = (current.astype(jnp.float32) - factor * update).astype(jnp.bfloat16)
    weights_next = lax.all_gather(fresh_rows, "shard", axis=1, tiled=True)
    whole = lax.psum(power, ("shard", "tensor"))
    basis_next = newton_schulz(whole, width)
    return (weights_next, basis_next, moment_one, moment_two)


PLAIN = ((1,), (0,))
BOTH_LAST = ((1,), (1,))


class Place:
    def __init__(self):
        tensor, self.z = lax.axis_index("tensor"), lax.axis_index("shard")
        self.core, self.y = lax.rem(tensor, 2), lax.div(tensor, 2)
        self.inner = lax.div(lax.rem(self.z + 1, 4), 2)

    def keeps(self, j):
        return jnp.where(self.inner == 1, 1 + j, 3 * j)

    def gives(self, j):
        return jnp.where(self.inner == 1, 3 * j, 1 + j)

    def layer(self, turn):
        return self.core if turn else 1 - self.core

    def piece(self, h, k, piece):
        return pl.multiple_of((h * 4 + (self.y ^ (k // 2)) * 2 + (self.inner ^ (k % 2))) * piece, piece)


def split(x):
    high = x.astype(jnp.bfloat16)
    return high, (x - high.astype(jnp.float32)).astype(jnp.bfloat16)


def dot3(a, b, dims=PLAIN):
    dot = lambda p, q: lax.dot_general(p, q, (dims, ((), ())), preferred_element_type=jnp.float32)
    return dot(a[0], b[0]) + (dot(a[0], b[1]) + dot(a[1], b[0]))


def params(megabytes):
    return pltpu.CompilerParams(vmem_limit_bytes=megabytes * 2**20)


def in_vmem(*arrays):
    return [pltpu.with_memory_space_constraint(x, pltpu.VMEM) for x in arrays]


def local_call(kernel, outs, *operands, name, scratch=(), flops=0):
    vmem = pl.BlockSpec(memory_space=pltpu.VMEM)
    return pl.pallas_call(
        kernel,
        out_shape=[pltpu.VMEM(shape, dtype) for shape, dtype in outs],
        in_specs=[vmem] * len(operands),
        out_specs=[vmem] * len(outs),
        scratch_shapes=scratch,
        compiler_params=params(12),
        cost_estimate=cost(flops),
        name=name,
    )(*in_vmem(*operands))


def cost(flops):
    return pl.CostEstimate(flops=int(flops), bytes_accessed=0, transcendentals=0) if flops else None


SPAN = 250.0


def encode(x):
    bound = jnp.max(jnp.abs(x), axis=0, keepdims=True)
    bound = (bound * 1.01 + 1e-30).astype(jnp.bfloat16).astype(jnp.float32)
    size = jnp.exp2(jnp.abs(x) * (SPAN / bound) - SPAN / 2)
    code = jnp.where(x < 0, -size, size)
    return code.astype(jnp.bfloat16), jnp.broadcast_to(bound, (16, x.shape[1])).astype(jnp.bfloat16)


def decode(code, bound):
    code, bound = code.astype(jnp.float32), bound[0:1].astype(jnp.float32)
    size = (jnp.log2(jnp.abs(code)) + SPAN / 2) * (bound / SPAN)
    return jnp.where(code < 0, -size, size)


def give_kernel(rows, grads_ref, *rest):
    outs, sems = rest[:-1], rest[-1]
    place = Place()
    copies = []
    for i in range(4):
        start = pl.multiple_of(place.gives(i % 2) * rows, rows)
        out = outs[0].at[pl.ds(i * rows, rows)] if i < 2 else outs[i - 1]
        copies.append(pltpu.make_async_copy(grads_ref.at[0, place.layer(i // 2), pl.ds(start, rows)], out, sems.at[i]))
    for copy in copies:
        copy.start()
    for copy in copies:
        copy.wait()


def give_blocks(grads, rows):
    heights = (2 * rows, rows, rows)
    return pl.pallas_call(
        functools.partial(give_kernel, rows),
        out_shape=[pltpu.VMEM((height, grads.shape[3]), grads.dtype) for height in heights],
        in_specs=[pl.BlockSpec(memory_space=pltpu.HBM)],
        out_specs=[pl.BlockSpec(memory_space=pltpu.VMEM)] * len(heights),
        scratch_shapes=[pltpu.SemaphoreType.DMA((4,))],
        compiler_params=params(4),
        name="give_blocks",
    )(pltpu.with_memory_space_constraint(grads, pltpu.HBM))


def prepare_kernel(basis_hbm, high_ref, low_ref, buffer, sems):
    layers = buffer.shape[0]
    copies = [pltpu.make_async_copy(basis_hbm.at[layer], buffer.at[layer], sems.at[layer]) for layer in range(layers)]
    for copy in copies:
        copy.start()
    for layer, copy in enumerate(copies):
        copy.wait()
        high_ref[layer], low_ref[layer] = split(buffer[layer])


def prepare_basis(basis):
    layers = basis.shape[0]
    vmem = pl.BlockSpec(memory_space=pltpu.VMEM)
    return pl.pallas_call(
        prepare_kernel,
        out_shape=[pltpu.VMEM(basis.shape, jnp.bfloat16)] * 2,
        in_specs=[pl.BlockSpec(memory_space=pltpu.HBM)],
        out_specs=[vmem] * 2,
        scratch_shapes=[pltpu.VMEM(basis.shape, jnp.float32), pltpu.SemaphoreType.DMA((layers,))],
        compiler_params=params(12),
        cost_estimate=cost(3e9),
        name="prepare_basis",
    )(pltpu.with_memory_space_constraint(basis, pltpu.HBM))


def kept_sum(place, grads_ref, other, turn, j, rows):
    start = pl.multiple_of(place.keeps(j) * rows, rows)
    kept = grads_ref[0, place.layer(turn), pl.ds(start, rows)]
    return kept.astype(jnp.float32) + other.astype(jnp.float32)


def project_kernel(turn, blocks, rows, grads_ref, other_ref, high_ref, low_ref, out_ref, code_ref):
    place = Place()
    basis = high_ref[place.layer(turn)], low_ref[place.layer(turn)]
    for i, j in enumerate(blocks):
        total = kept_sum(place, grads_ref, other_ref[i * rows : (i + 1) * rows], turn, j, rows)
        projected = dot3(split(total), basis)
        out_ref[i * rows : (i + 1) * rows] = projected
        row = i * (rows + 16)
        code_ref[row : row + rows], code_ref[row + rows : row + rows + 16] = encode(projected)


def project(grads, other, basis, turn, blocks):
    rank, rows = basis[0].shape[2], other.shape[0] // len(blocks)
    kernel = functools.partial(project_kernel, turn, blocks, rows)
    outs = [((len(blocks) * rows, rank), jnp.float32), ((len(blocks) * (rows + 16), rank), jnp.bfloat16)]
    return local_call(kernel, outs, grads, other, *basis, name="project")


HALVES = 2


def power_kernel(turn, scale, grads_ref, first_ref, second_ref, *refs):
    place = Place()
    parts = 1 + turn
    others, partials, received, rest = refs[:parts], refs[parts : 2 * parts], refs[2 * parts : 3 * parts], refs[3 * parts :]
    rest = rest[3 * turn :]
    half0_ref, half1_ref, one_ref, two_ref, code_ref, product, one, two, sems = rest
    layers, rows = first_ref.shape[0], first_ref.shape[1]
    sums, summed = [], []
    for j in range(2):
        part, row = (0, j) if turn == 0 else (j, 0)
        block, coded = pl.ds(row * rows, rows), row * (rows + 16)
        summed.append(kept_sum(place, grads_ref, others[part][block], turn, j, rows))
        code, bound = received[part][coded : coded + rows], received[part][coded + rows : coded + rows + 16]
        sums.append(partials[part][block] + decode(code, bound))
    layer = place.layer(turn)
    reduced = scale * jnp.where(place.z < 2, sums[0], sums[1])
    one[...], two[...], direction = adam_direction(reduced, first_ref[layer], second_ref[layer])
    copies = [pltpu.make_async_copy(x, out.at[layer], sems.at[i]) for i, (x, out) in enumerate(((one, one_ref), (two, two_ref)))]
    for copy in copies:
        copy.start()
    if turn == 0:
        code_ref[0:rows], code_ref[rows:] = encode(direction)
    else:
        code_ref[1 - layer] = refs[3 * parts + 2][...]
        code_ref[layer, 0:rows], code_ref[layer, rows:] = encode(direction)
    product[...] = dot3(split(jnp.concatenate(sums).T), split(jnp.concatenate(summed)))
    piece = product.shape[0] // (4 * HALVES)
    for h in range(HALVES):
        for k in range(4):
            (half0_ref, half1_ref)[h][pl.ds(k * piece, piece)] = product[pl.ds(place.piece(h, k, piece), piece)]
    for copy in copies:
        copy.wait()


def power_product(grads, first_moment, second_moment, others, partials, received, turn, scale, before=()):
    width = grads.shape[3]
    layers, rows, rank = first_moment.shape
    vmem, anywhere = pl.BlockSpec(memory_space=pltpu.VMEM), pl.BlockSpec(memory_space=pl.ANY)
    operands = in_vmem(grads, first_moment, second_moment, *others, *partials, *received)
    count = len(operands)
    return pl.pallas_call(
        functools.partial(power_kernel, turn, scale),
        out_shape=[pltpu.VMEM((rank // HALVES, width), jnp.float32)] * HALVES
        + [jax.ShapeDtypeStruct(first_moment.shape, jnp.float32)] * 2
        + [pltpu.VMEM((layers, rows + 16, rank) if turn else (rows + 16, rank), jnp.bfloat16)],
        in_specs=[vmem] * count + [anywhere, anywhere, vmem][: len(before)],
        out_specs=[vmem] * HALVES + [anywhere] * 2 + [vmem],
        scratch_shapes=[pltpu.VMEM((rank, width), jnp.float32)]
        + [pltpu.VMEM((rows, rank), jnp.float32)] * 2
        + [pltpu.SemaphoreType.DMA((2,))],
        input_output_aliases={count: HALVES, count + 1: HALVES + 1} if before else {},
        compiler_params=params(12),
        cost_estimate=cost(5e9 * turn),
        name="power",
    )(*operands, *before[:2], *in_vmem(*before[2:]))


def add_split_kernel(own_ref, received_ref, keep_ref, give_ref):
    half = keep_ref.shape[0]
    keep_ref[...] = own_ref[0:half] + received_ref[0:half]
    give_ref[...] = own_ref[half:] + received_ref[half:]


def add_split(own, received):
    outs = [((own.shape[0] // 2, own.shape[1]), jnp.float32)] * 2
    return local_call(add_split_kernel, outs, own, received, name="add_split", flops=1e9)


def add_kernel(own_ref, received_ref, out_ref):
    out_ref[...] = own_ref[...] + received_ref[...]


def join_kernel(own_ref, received_ref, out_ref):
    half = own_ref.shape[0]
    out_ref[0:half] = own_ref[...]
    out_ref[half:] = received_ref[...]


def add(own, received):
    return local_call(add_kernel, [(own.shape, jnp.float32)], own, received, name="add")[0]


def join(own, received):
    outs = [((2 * own.shape[0], own.shape[1]), jnp.float32)]
    return local_call(join_kernel, outs, own, received, name="join")[0]


def newton_schulz_kernel(*refs):
    place = Place()
    parts, (out_ref, result_ref, power_ref, sems) = refs[:-4], refs[-4:]
    piece = parts[0].shape[0] // 2
    for h in range(HALVES):
        for k in range(4):
            part = parts[2 * h + k // 2]
            power_ref[pl.ds(place.piece(h, k, piece), piece)] = part[pl.ds(k % 2 * piece, piece)]
    power = power_ref[...]
    rank, width = power.shape
    unscaled = split(power)
    scale = 1.0 / (jnp.sqrt(jnp.sum(power * power)) + norm_eps)
    gram = dot3(unscaled, unscaled, BOTH_LAST) * scale * scale
    ident = lax.broadcasted_iota(jnp.int32, gram.shape, 0) == lax.broadcasted_iota(jnp.int32, gram.shape, 1)
    diagonal = jnp.where(ident, coeff_a, 0.0)
    product = None
    for sweep in range(NS_ITERS - 1):
        g = split(gram)
        factor = diagonal + coeff_b * gram + coeff_c * dot3(g, g)
        f = split(factor)
        gram = dot3(split(dot3(f, g)), f)
        product = f if product is None else split(dot3(product, f))
    iterate = split(dot3(product, unscaled))
    g = split(gram)
    last = split((diagonal + coeff_b * gram + coeff_c * dot3(g, g)) * (scale * width**0.5))
    copies = []
    for i in range(width // rank):
        columns = slice(i * rank, (i + 1) * rank)
        result_ref[columns] = dot3(last, [term[:, columns] for term in iterate]).T
        copies.append(pltpu.make_async_copy(result_ref.at[columns], out_ref.at[place.core, columns], sems.at[i]))
        copies[-1].start()
    for copy in copies:
        copy.wait()


def newton_schulz_power(layers, *parts):
    rank, width = 2 * HALVES * parts[0].shape[0], parts[0].shape[1]
    vmem = pl.BlockSpec(memory_space=pltpu.VMEM)
    return pl.pallas_call(
        newton_schulz_kernel,
        out_shape=[jax.ShapeDtypeStruct((layers, width, rank), jnp.float32), pltpu.VMEM((width, rank), jnp.float32)],
        in_specs=[vmem] * len(parts),
        out_specs=[pl.BlockSpec(memory_space=pl.ANY), vmem],
        scratch_shapes=[pltpu.VMEM((rank, width), jnp.float32), pltpu.SemaphoreType.DMA((width // rank,))],
        compiler_params=params(12),
        cost_estimate=cost(4e9),
        name="newton_schulz",
    )(*in_vmem(*parts))


def put_layer_kernel(layer_ref, whole_ref, out_ref, sems):
    count = sems.shape[0]
    rows = layer_ref.shape[0] // count
    copies = []
    for i in range(count):
        part = pl.ds(i * rows, rows)
        copies.append(pltpu.make_async_copy(layer_ref.at[part], out_ref.at[1 - Place().core, part], sems.at[i]))
    for copy in copies:
        copy.start()
    for copy in copies:
        copy.wait()


def put_layer(layer, whole):
    hbm = pl.BlockSpec(memory_space=pl.ANY)
    return pl.pallas_call(
        put_layer_kernel,
        out_shape=jax.ShapeDtypeStruct(whole.shape, whole.dtype),
        in_specs=[pl.BlockSpec(memory_space=pltpu.VMEM), hbm],
        out_specs=hbm,
        scratch_shapes=[pltpu.SemaphoreType.DMA((4,))],
        input_output_aliases={1: 0},
        compiler_params=params(4),
        name="put_layer",
    )(*in_vmem(layer), whole)


def update_kernel(factor, index_ref, weights_ref, basis_ref, *refs):
    directions, (out_ref, high, low) = refs[:2], refs[-3:]
    k = pl.program_id(1)

    @pl.when(k == 0)
    def _():
        high[...], low[...] = split(basis_ref[0].T)

    for step, direction in enumerate(directions):

        @pl.when(k == step)
        def _(direction=direction):
            rows = out_ref.shape[1]
            exact = decode(direction[0, 0:rows], direction[0, rows:])
            update = dot3(split(exact), (high[...], low[...]))
            out_ref[0] = (weights_ref[0].astype(jnp.float32) - factor * update).astype(out_ref.dtype)


def update_weights(index, weights, basis, blocks, directions, factor, before=()):
    layers, height, width = weights.shape
    rank, rows = basis.shape[2], height // 4
    row_block = pl.BlockSpec((1, rows, width), lambda l, k, index: (l, index[0] ^ (blocks[0] + k * (blocks[1] - blocks[0])), 0))
    layer_block = lambda a, b: pl.BlockSpec((1, a, b), lambda l, k, index: (l, 0, 0))
    return pl.pallas_call(
        functools.partial(update_kernel, factor),
        out_shape=jax.ShapeDtypeStruct(weights.shape, weights.dtype),
        grid_spec=pltpu.PrefetchScalarGridSpec(
            num_scalar_prefetch=1,
            grid=(layers, 2),
            in_specs=[row_block, layer_block(width, rank)]
            + [layer_block(rows + 16, rank)] * 2
            + [pl.BlockSpec(memory_space=pl.ANY)] * len(before),
            out_specs=row_block,
            scratch_shapes=[pltpu.VMEM((rank, width), jnp.bfloat16)] * 2,
        ),
        input_output_aliases={5: 0} if before else {},
        compiler_params=params(12),
        cost_estimate=cost(3e9),
        name="update_weights",
    )(index, pltpu.with_memory_space_constraint(weights, pltpu.HBM), basis, *directions, *before)


def xor_pairs(k):
    return [(i, i ^ k) for i in range(4)]


def over_z(x, k):
    return lax.ppermute(x, "shard", xor_pairs(k))


def over_core(x):
    return lax.ppermute(x, "tensor", xor_pairs(1))


def over_y(x):
    return lax.ppermute(x, "tensor", xor_pairs(2))


class Order:
    def __init__(self):
        self.last = None

    def step(self, *operands):
        if self.last is None:
            return operands
        return lax.optimization_barrier(tuple(operands) + (self.last,))[:-1]

    def through(self, result):
        self.last = result
        return result


def line_body(grads, weights, basis, first_moment, second_moment):
    width = basis.shape[1]
    scale_factor = width ** (-0.5)
    layers, rows = grads.shape[1], first_moment.shape[1]
    order = Order()

    others = [over_z(block, 1) for block in give_blocks(grads, rows)]
    high, low = prepare_basis(basis)
    partials, received = [], []

    def exchange(i, turn, blocks, *awaited):
        other, *awaited = order.step(others[i], *awaited)
        partial, code = project(grads, other, (high, low), turn, blocks)
        partials.append(order.through(partial))
        received.append(over_z(code, 3))
        return awaited

    def product(turn, *before):
        some = slice(1, 3) if turn else slice(0, 1)
        operands = order.step(*others[some], *partials[some], *received[some])
        n = 1 + turn
        *halves, one, two, code = power_product(
            grads, first_moment, second_moment, operands[:n], operands[n : 2 * n], operands[2 * n :], turn, scale_factor, before
        )
        order.through(halves[0])
        return halves, (one, two, code)

    def scatter(over, x, received):
        keep, give = add_split(*order.step(x, received))
        return order.through(keep), over(give)

    def total(over, x, received):
        x = order.through(add(*order.step(x, received)))
        return x, over(x)

    def gather(over, x, received):
        x = order.through(join(*order.step(x, received)))
        return x, over(x)

    next_z = lambda x: over_z(x, 1)
    opposite_z = lambda x: over_z(x, 3)

    exchange(0, 0, (0, 1))
    exchange(1, 1, (0,))
    gifts, before = product(0)
    gifts = [over_core(gift) for gift in gifts]
    (received[1],) = exchange(2, 1, (1,), received[1])
    parts, (moment_one, moment_two, code) = product(1, *before)
    parts = [scatter(over_y, part, gift) for part, gift in zip(parts, gifts)]
    (code,) = order.step(code)
    near, opposite = next_z(code), opposite_z(code)
    first = scatter(next_z, *parts[0])
    near, opposite, *second = order.step(near, opposite, *parts[1])
    parts = [first, scatter(next_z, *second)]
    parts = [total(opposite_z, *part) for part in parts]
    parts = [total(next_z, *part) for part in parts]
    last = next_z(order.step(opposite)[0])
    parts = [gather(over_y, *part) for part in parts]
    index = lax.axis_index("shard").astype(jnp.int32)[None]
    factor = learn_rate * galore_scale * scale_factor
    update = functools.partial(update_weights, index, weights, basis)
    weights_next = order.through(update((0, 1), order.step(code, near), factor))
    last, *parts = order.step(last, *[x for part in parts for x in part])
    basis_next, own = newton_schulz_power(layers, *parts)
    order.through(own)
    other = over_core(own)
    weights_next = order.through(update((2, 3), order.step(last, opposite), factor, (weights_next,)))
    basis_next = put_layer(*order.step(other, basis_next))
    return (weights_next, basis_next, moment_one, moment_two)


def solution(mesh):
    line = mesh.shape["shard"] == 4 and mesh.shape["tensor"] == 4

    def body(grads, *others):
        return (line_body if line and grads.shape[1] == 2 else general_body)(grads, *others)

    return jax.shard_map(
        body,
        mesh=mesh,
        in_specs=(
            P("shard", "section", "tensor", None),
            P("section", "tensor", None),
            P("section", None, None),
            P("section", ("tensor", "shard"), None),
            P("section", ("tensor", "shard"), None),
        ),
        out_specs=(
            P("section", "tensor", None),
            P("section", None, None),
            P("section", ("tensor", "shard"), None),
            P("section", ("tensor", "shard"), None),
        ),
        check_vma=False,
    )
```

```python
import functools

import jax
import jax.numpy as jnp
from jax import lax
from jax.experimental import pallas as pl
from jax.experimental.pallas import tpu as pltpu
from jax.sharding import PartitionSpec as P

NS_ITERS = 3
STEP = 1000


learn_rate = 0.5
galore_scale = 0.25
beta_one = 0.9
beta_two = 0.999
adam_eps = 1e-08
norm_eps = 1e-07
coeff_a = 3.4445
coeff_b = -4.775
coeff_c = 2.0315
highest = lax.Precision.HIGHEST


def newton_step(iterate, gram_matrix):
    squared = jnp.einsum("lrs,lst->lrt", gram_matrix, gram_matrix, precision=highest)
    mixing = coeff_b * gram_matrix + coeff_c * squared
    return coeff_a * iterate + jnp.einsum("ldr,lrs->lds", iterate, mixing, precision=highest)


def adam_direction(reduced, first_moment, second_moment):
    moment_one = beta_one * first_moment + (1.0 - beta_one) * reduced
    moment_two = beta_two * second_moment + (1.0 - beta_two) * reduced * reduced
    corrected_one = moment_one / (1.0 - beta_one**STEP)
    corrected_two = moment_two / (1.0 - beta_two**STEP)
    return (moment_one, moment_two, corrected_one / (jnp.sqrt(corrected_two) + adam_eps))


def newton_schulz(power, width):
    norms = jnp.sqrt(jnp.sum(power * power, axis=(1, 2)))
    iterate = power / (norms + norm_eps)[:, None, None]
    for sweep in range(NS_ITERS):
        gram_matrix = jnp.einsum("ldr,lds->lrs", iterate, iterate, precision=highest)
        iterate = newton_step(iterate, gram_matrix)
    return width**0.5 * iterate


def general_body(grads, weights, basis, first_moment, second_moment):
    width = basis.shape[1]
    scale_factor = width ** (-0.5)
    local_grads = grads[0]
    block_rows = first_moment.shape[1]
    summed = lax.psum_scatter(
        local_grads.astype(jnp.float32), "shard", scatter_dimension=1, tiled=True
    )
    projected = jnp.einsum("lfd,ldr->lfr", summed, basis, precision=highest)
    power = jnp.einsum("lfd,lfr->ldr", summed, projected, precision=highest)
    reduced = scale_factor * projected
    moment_one, moment_two, direction = adam_direction(reduced, first_moment, second_moment)
    factor = learn_rate * galore_scale * scale_factor
    own_start = lax.axis_index("shard") * block_rows
    current = lax.dynamic_slice_in_dim(weights, own_start, block_rows, 1)
    update = jnp.einsum("lfr,ldr->lfd", direction, basis, precision=highest)
    fresh_rows = (current.astype(jnp.float32) - factor * update).astype(jnp.bfloat16)
    weights_next = lax.all_gather(fresh_rows, "shard", axis=1, tiled=True)
    whole = lax.psum(power, ("shard", "tensor"))
    basis_next = newton_schulz(whole, width)
    return (weights_next, basis_next, moment_one, moment_two)


PLAIN = ((1,), (0,))
BOTH_LAST = ((1,), (1,))


class Place:
    def __init__(self):
        tensor, self.z = lax.axis_index("tensor"), lax.axis_index("shard")
        self.core, self.y = lax.rem(tensor, 2), lax.div(tensor, 2)
        self.inner = lax.div(lax.rem(self.z + 1, 4), 2)

    def keeps(self, j):
        return jnp.where(self.inner == 1, 1 + j, 3 * j)

    def gives(self, j):
        return jnp.where(self.inner == 1, 3 * j, 1 + j)

    def layer(self, turn):
        return self.core if turn else 1 - self.core

    def piece(self, h, k, piece):
        return pl.multiple_of((h * 4 + (self.y ^ (k // 2)) * 2 + (self.inner ^ (k % 2))) * piece, piece)


def split(x):
    high = x.astype(jnp.bfloat16)
    return high, (x - high.astype(jnp.float32)).astype(jnp.bfloat16)


def dot3(a, b, dims=PLAIN):
    dot = lambda p, q: lax.dot_general(p, q, (dims, ((), ())), preferred_element_type=jnp.float32)
    return dot(a[0], b[0]) + (dot(a[0], b[1]) + dot(a[1], b[0]))


def params(megabytes):
    return pltpu.CompilerParams(vmem_limit_bytes=megabytes * 2**20)


def in_vmem(*arrays):
    return [pltpu.with_memory_space_constraint(x, pltpu.VMEM) for x in arrays]


def local_call(kernel, outs, *operands, name, scratch=(), flops=0):
    vmem = pl.BlockSpec(memory_space=pltpu.VMEM)
    return pl.pallas_call(
        kernel,
        out_shape=[pltpu.VMEM(shape, dtype) for shape, dtype in outs],
        in_specs=[vmem] * len(operands),
        out_specs=[vmem] * len(outs),
        scratch_shapes=scratch,
        compiler_params=params(12),
        cost_estimate=cost(flops),
        name=name,
    )(*in_vmem(*operands))


def cost(flops):
    return pl.CostEstimate(flops=int(flops), bytes_accessed=0, transcendentals=0) if flops else None


SPAN = 250.0


def encode(x):
    bound = jnp.max(jnp.abs(x), axis=0, keepdims=True)
    bound = (bound * 1.01 + 1e-30).astype(jnp.bfloat16).astype(jnp.float32)
    size = jnp.exp2(jnp.abs(x) * (SPAN / bound) - SPAN / 2)
    code = jnp.where(x < 0, -size, size)
    return code.astype(jnp.bfloat16), jnp.broadcast_to(bound, (16, x.shape[1])).astype(jnp.bfloat16)


def decode(code, bound):
    code, bound = code.astype(jnp.float32), bound[0:1].astype(jnp.float32)
    size = (jnp.log2(jnp.abs(code)) + SPAN / 2) * (bound / SPAN)
    return jnp.where(code < 0, -size, size)


def prepare_kernel(basis_hbm, high_ref, low_ref, buffer, sems):
    layers = buffer.shape[0]
    copies = [pltpu.make_async_copy(basis_hbm.at[layer], buffer.at[layer], sems.at[layer]) for layer in range(layers)]
    for copy in copies:
        copy.start()
    for layer, copy in enumerate(copies):
        copy.wait()
        high_ref[layer], low_ref[layer] = split(buffer[layer])


def prepare_basis(basis):
    layers = basis.shape[0]
    vmem = pl.BlockSpec(memory_space=pltpu.VMEM)
    return pl.pallas_call(
        prepare_kernel,
        out_shape=[pltpu.VMEM(basis.shape, jnp.bfloat16)] * 2,
        in_specs=[pl.BlockSpec(memory_space=pltpu.HBM)],
        out_specs=[vmem] * 2,
        scratch_shapes=[pltpu.VMEM(basis.shape, jnp.float32), pltpu.SemaphoreType.DMA((layers,))],
        compiler_params=params(12),
        cost_estimate=cost(3e9),
        name="prepare_basis",
    )(pltpu.with_memory_space_constraint(basis, pltpu.HBM))


def fetch_kernel(weights_hbm, high_ref, low_ref, weights_ref, high_t_ref, low_t_ref, sems):
    layers = weights_ref.shape[0]
    copies = [pltpu.make_async_copy(weights_hbm.at[layer], weights_ref.at[layer], sems.at[layer]) for layer in range(layers)]
    for copy in copies:
        copy.start()
    for layer in range(layers):
        for source, out in ((high_ref, high_t_ref), (low_ref, low_t_ref)):
            out[layer] = source[layer].astype(jnp.float32).T.astype(jnp.bfloat16)
    for copy in copies:
        copy.wait()


def fetch(weights, high, low):
    layers, width, rank = high.shape
    vmem = pl.BlockSpec(memory_space=pltpu.VMEM)
    return pl.pallas_call(
        fetch_kernel,
        out_shape=[pltpu.VMEM(weights.shape, weights.dtype)] + [pltpu.VMEM((layers, rank, width), jnp.bfloat16)] * 2,
        in_specs=[pl.BlockSpec(memory_space=pltpu.HBM), vmem, vmem],
        out_specs=[vmem] * 3,
        scratch_shapes=[pltpu.SemaphoreType.DMA((layers,))],
        compiler_params=params(12),
        name="fetch",
    )(pltpu.with_memory_space_constraint(weights, pltpu.HBM), *in_vmem(high, low))


def code_blocks(code_ref, parts):
    for j, part in enumerate(parts):
        rows = part.shape[0]
        row = j * (rows + 16)
        code_ref[row : row + rows], code_ref[row + rows : row + rows + 16] = encode(part)


def blocks_of(code_ref):
    rows = code_ref.shape[0] // 2 - 16
    return [decode(code_ref[j * (rows + 16) : j * (rows + 16) + rows], code_ref[j * (rows + 16) + rows : (j + 1) * (rows + 16)]) for j in range(2)]


def rows_of(grads_ref, layer, block, rows):
    return grads_ref[0, layer, pl.ds(pl.multiple_of(block * rows, rows), rows)]


def exact_dot(a, b, dims=PLAIN):
    dot = lambda p, q: lax.dot_general(p, q, (dims, ((), ())), preferred_element_type=jnp.float32)
    return dot(a[0], b) + dot(a[1], b) if isinstance(a, tuple) else dot(a, b[0]) + dot(a, b[1])


def project_kernel(turn, grads_ref, high_ref, low_ref, out_ref, code_ref):
    place = Place()
    layer, rows = place.layer(turn), out_ref.shape[0] // 2
    basis = high_ref[layer], low_ref[layer]
    code_blocks(code_ref, [exact_dot(rows_of(grads_ref, layer, place.gives(j), rows), basis) for j in range(2)])
    for j in range(2):
        out_ref[j * rows : (j + 1) * rows] = exact_dot(rows_of(grads_ref, layer, place.keeps(j), rows), basis)


def project(grads, basis, turn):
    rows, rank = grads.shape[2] // 4, basis[0].shape[2]
    outs = [((2 * rows, rank), jnp.float32), ((2 * (rows + 16), rank), jnp.bfloat16)]
    return local_call(functools.partial(project_kernel, turn), outs, grads, *basis, name="project")


def add_coded_kernel(own_ref, received_ref, out_ref, code_ref):
    rows = own_ref.shape[0] // 2
    parts = [own_ref[j * rows : (j + 1) * rows] + block for j, block in enumerate(blocks_of(received_ref))]
    code_blocks(code_ref, parts)
    for j, part in enumerate(parts):
        out_ref[j * rows : (j + 1) * rows] = part


def add_coded(own, received):
    outs = [(own.shape, jnp.float32), (received.shape, jnp.bfloat16)]
    return local_call(add_coded_kernel, outs, own, received, name="add_coded")


HALVES = 2


def power_kernel(turn, scale, grads_ref, first_ref, second_ref, kept_ref, given_ref, *rest):
    place = Place()
    code_before = rest[2] if turn else None
    half0_ref, half1_ref, one_ref, two_ref, code_ref, product, one, two, sems = rest[3 * turn :]
    rows = first_ref.shape[1]
    sums = [kept_ref[0:rows], kept_ref[rows:]]
    layer = place.layer(turn)
    reduced = scale * jnp.where(place.z < 2, sums[0], sums[1])
    one[...], two[...], direction = adam_direction(reduced, first_ref[layer], second_ref[layer])
    copies = [pltpu.make_async_copy(x, out.at[layer], sems.at[i]) for i, (x, out) in enumerate(((one, one_ref), (two, two_ref)))]
    for copy in copies:
        copy.start()
    if turn == 0:
        code_ref[0:rows], code_ref[rows:] = encode(direction)
    else:
        code_ref[1 - layer] = code_before[...]
        code_ref[layer, 0:rows], code_ref[layer, rows:] = encode(direction)
    blocks = [place.keeps(0), place.keeps(1), place.gives(0), place.gives(1)]
    rows_in_order = jnp.concatenate([rows_of(grads_ref, layer, block, rows) for block in blocks])
    product[...] = exact_dot(split(jnp.concatenate(sums + blocks_of(given_ref)).T), rows_in_order)
    piece = product.shape[0] // (4 * HALVES)
    for h in range(HALVES):
        for k in range(4):
            (half0_ref, half1_ref)[h][pl.ds(k * piece, piece)] = product[pl.ds(place.piece(h, k, piece), piece)]
    for copy in copies:
        copy.wait()


def power_product(grads, first_moment, second_moment, kept, given, turn, scale, before=()):
    width = grads.shape[3]
    layers, rows, rank = first_moment.shape
    vmem, anywhere = pl.BlockSpec(memory_space=pltpu.VMEM), pl.BlockSpec(memory_space=pl.ANY)
    operands = in_vmem(grads, first_moment, second_moment, kept, given)
    count = len(operands)
    return pl.pallas_call(
        functools.partial(power_kernel, turn, scale),
        out_shape=[pltpu.VMEM((rank // HALVES, width), jnp.float32)] * HALVES
        + [jax.ShapeDtypeStruct(first_moment.shape, jnp.float32)] * 2
        + [pltpu.VMEM((layers, rows + 16, rank) if turn else (rows + 16, rank), jnp.bfloat16)],
        in_specs=[vmem] * count + [anywhere, anywhere, vmem][: len(before)],
        out_specs=[vmem] * HALVES + [anywhere] * 2 + [vmem],
        scratch_shapes=[pltpu.VMEM((rank, width), jnp.float32)]
        + [pltpu.VMEM((rows, rank), jnp.float32)] * 2
        + [pltpu.SemaphoreType.DMA((2,))],
        input_output_aliases={count: HALVES, count + 1: HALVES + 1} if before else {},
        compiler_params=params(12),
        cost_estimate=cost(5e9),
        name="power",
    )(*operands, *before[:2], *in_vmem(*before[2:]))


def add_split_kernel(own_ref, received_ref, keep_ref, give_ref):
    half = keep_ref.shape[0]
    keep_ref[...] = own_ref[0:half] + received_ref[0:half]
    give_ref[...] = own_ref[half:] + received_ref[half:]


def add_split(own, received, flops):
    outs = [((own.shape[0] // 2, own.shape[1]), jnp.float32)] * 2
    return local_call(add_split_kernel, outs, own, received, name="add_split", flops=flops)


def add_kernel(own_ref, received_ref, out_ref):
    out_ref[...] = own_ref[...] + received_ref[...]


def join_kernel(own_ref, received_ref, out_ref):
    half = own_ref.shape[0]
    out_ref[0:half] = own_ref[...]
    out_ref[half:] = received_ref[...]


def add(own, received, flops):
    return local_call(add_kernel, [(own.shape, jnp.float32)], own, received, name="add", flops=flops)[0]


def join(own, received):
    outs = [((2 * own.shape[0], own.shape[1]), jnp.float32)]
    return local_call(join_kernel, outs, own, received, name="join")[0]


def newton_schulz_kernel(*refs):
    place = Place()
    parts, (out_ref, result_ref, power_ref, sems) = refs[:-4], refs[-4:]
    piece = parts[0].shape[0] // 2
    for h in range(HALVES):
        for k in range(4):
            part = parts[2 * h + k // 2]
            power_ref[pl.ds(place.piece(h, k, piece), piece)] = part[pl.ds(k % 2 * piece, piece)]
    power = power_ref[...]
    rank, width = power.shape
    unscaled = split(power)
    scale = 1.0 / (jnp.sqrt(jnp.sum(power * power)) + norm_eps)
    gram = dot3(unscaled, unscaled, BOTH_LAST) * scale * scale
    ident = lax.broadcasted_iota(jnp.int32, gram.shape, 0) == lax.broadcasted_iota(jnp.int32, gram.shape, 1)
    diagonal = jnp.where(ident, coeff_a, 0.0)
    product = None
    for sweep in range(NS_ITERS - 1):
        g = split(gram)
        factor = diagonal + coeff_b * gram + coeff_c * dot3(g, g)
        f = split(factor)
        gram = dot3(split(dot3(f, g)), f)
        product = f if product is None else split(dot3(product, f))
    iterate = split(dot3(product, unscaled))
    g = split(gram)
    last = split((diagonal + coeff_b * gram + coeff_c * dot3(g, g)) * (scale * width**0.5))
    copies = []
    for i in range(width // rank):
        columns = slice(i * rank, (i + 1) * rank)
        result_ref[columns] = dot3(last, [term[:, columns] for term in iterate]).T
        copies.append(pltpu.make_async_copy(result_ref.at[columns], out_ref.at[place.core, columns], sems.at[i]))
        copies[-1].start()
    for copy in copies:
        copy.wait()


def newton_schulz_power(layers, *parts):
    rank, width = 2 * HALVES * parts[0].shape[0], parts[0].shape[1]
    vmem = pl.BlockSpec(memory_space=pltpu.VMEM)
    return pl.pallas_call(
        newton_schulz_kernel,
        out_shape=[jax.ShapeDtypeStruct((layers, width, rank), jnp.float32), pltpu.VMEM((width, rank), jnp.float32)],
        in_specs=[vmem] * len(parts),
        out_specs=[pl.BlockSpec(memory_space=pl.ANY), vmem],
        scratch_shapes=[pltpu.VMEM((rank, width), jnp.float32), pltpu.SemaphoreType.DMA((width // rank,))],
        compiler_params=params(12),
        name="newton_schulz",
    )(*in_vmem(*parts))


def put_layer_kernel(layer_ref, whole_ref, out_ref, sems):
    count = sems.shape[0]
    rows = layer_ref.shape[0] // count
    copies = []
    for i in range(count):
        part = pl.ds(i * rows, rows)
        copies.append(pltpu.make_async_copy(layer_ref.at[part], out_ref.at[1 - Place().core, part], sems.at[i]))
    for copy in copies:
        copy.start()
    for copy in copies:
        copy.wait()


def put_layer(layer, whole):
    hbm = pl.BlockSpec(memory_space=pl.ANY)
    return pl.pallas_call(
        put_layer_kernel,
        out_shape=jax.ShapeDtypeStruct(whole.shape, whole.dtype),
        in_specs=[pl.BlockSpec(memory_space=pltpu.VMEM), hbm],
        out_specs=hbm,
        scratch_shapes=[pltpu.SemaphoreType.DMA((4,))],
        input_output_aliases={1: 0},
        compiler_params=params(4),
        name="put_layer",
    )(*in_vmem(layer), whole)


def stack_kernel(a_ref, b_ref, out_ref):
    out_ref[0] = a_ref[...]
    out_ref[1] = b_ref[...]


def stack(a, b):
    return local_call(stack_kernel, [((2,) + a.shape, a.dtype)], a, b, name="stack")[0]


def update_kernel(factor, blocks, weights_ref, high_ref, low_ref, *refs):
    directions, (out_ref, buffer, sems) = refs[:2], refs[-3:]
    place = Place()
    layers, rows = weights_ref.shape[0], buffer.shape[2]
    copies = []
    for layer in range(layers):
        basis = high_ref[layer], low_ref[layer]
        for i, (direction, (k, source)) in enumerate(zip(directions, blocks)):
            where = pl.ds(pl.multiple_of((place.z ^ k) * rows, rows), rows)
            exact = decode(direction[source, layer, 0:rows], direction[source, layer, rows:])
            update = dot3(split(exact), basis)
            buffer[layer, i] = (weights_ref[layer, where].astype(jnp.float32) - factor * update).astype(buffer.dtype)
            copies.append(pltpu.make_async_copy(buffer.at[layer, i], out_ref.at[layer, where], sems.at[layer, i]))
            copies[-1].start()
    for copy in copies:
        copy.wait()


def update_weights(weights, basis, directions, blocks, factor, flops, before=()):
    layers, height, width = weights.shape
    vmem, anywhere = pl.BlockSpec(memory_space=pltpu.VMEM), pl.BlockSpec(memory_space=pl.ANY)
    operands = in_vmem(weights, *basis, *directions)
    return pl.pallas_call(
        functools.partial(update_kernel, factor, blocks),
        out_shape=jax.ShapeDtypeStruct(weights.shape, weights.dtype),
        in_specs=[vmem] * len(operands) + [anywhere] * len(before),
        out_specs=anywhere,
        scratch_shapes=[pltpu.VMEM((layers, 2, height // 4, width), weights.dtype), pltpu.SemaphoreType.DMA((layers, 2))],
        input_output_aliases={5: 0} if before else {},
        compiler_params=params(12),
        cost_estimate=cost(flops),
        name="update_weights",
    )(*operands, *before)


def xor_pairs(k):
    return [(i, i ^ k) for i in range(4)]


def over_z(x, k):
    return lax.ppermute(x, "shard", xor_pairs(k))


def over_core(x):
    return lax.ppermute(x, "tensor", xor_pairs(1))


def over_y(x):
    return lax.ppermute(x, "tensor", xor_pairs(2))


class Order:
    def __init__(self):
        self.last = None

    def step(self, *operands):
        if self.last is None:
            return operands
        return lax.optimization_barrier(tuple(operands) + (self.last,))[:-1]

    def through(self, result):
        self.last = result
        return result


def line_body(grads, weights, basis, first_moment, second_moment):
    width = basis.shape[1]
    scale_factor = width ** (-0.5)
    layers, rows = grads.shape[1], first_moment.shape[1]
    order = Order()

    high, low = prepare_basis(basis)

    def product(turn, kept, given, *before):
        *halves, one, two, code = power_product(
            grads, first_moment, second_moment, *order.step(kept, given), turn, scale_factor, before
        )
        order.through(halves[0])
        return halves, (one, two, code)

    def add_code(x, received):
        x, code = add_coded(*order.step(x, received))
        return order.through(x), code

    def scatter(over, x, received, flops=0):
        keep, give = add_split(*order.step(x, received), flops)
        return order.through(keep), over(give)

    def total(over, x, received, flops=0):
        x = order.through(add(*order.step(x, received), flops))
        return x, over(x)

    def gather(over, x, received):
        x = order.through(join(*order.step(x, received)))
        return x, over(x)

    next_z = lambda x: over_z(x, 1)
    opposite_z = lambda x: over_z(x, 3)

    codes = []
    kept = []
    for turn in range(2):
        x, code = project(order.step(grads)[0], (high, low), turn)
        kept.append(order.through(x))
        codes.append(code)
    first, code = add_code(kept[0], next_z(codes[0]))
    first = first, opposite_z(code)
    second, code = add_code(kept[1], next_z(order.step(codes[1])[0]))
    second = second, opposite_z(code)
    weights, *turned = fetch(*order.step(weights, high, low))
    order.through(weights)
    sums = []
    for pair in (first, second):
        x, code = add_code(*pair)
        sums.append((x, next_z(code)))
    gifts, before = product(0, *sums[0])
    gifts = [over_core(gift) for gift in gifts]
    parts, (moment_one, moment_two, code) = product(1, *sums[1], *before)
    parts = [scatter(over_y, part, gift, 1e9) for part, gift in zip(parts, gifts)]
    opposite = opposite_z(order.step(code)[0])
    parts = [scatter(next_z, *part) for part in parts]
    opposite, *parts[0] = order.step(opposite, *parts[0])
    first = total(opposite_z, *parts[0], 1e9)
    parts = [first, total(opposite_z, *parts[1])]
    parts = [total(next_z, *part) for part in parts]
    parts = [gather(over_y, *part) for part in parts]
    pair = next_z(order.through(stack(*order.step(code, opposite))))
    factor = learn_rate * galore_scale * scale_factor
    code, opposite, weights, *parts[0] = order.step(code[None], opposite[None], weights, *parts[0])
    weights_next = order.through(update_weights(weights, turned, (code, opposite), ((0, 0), (3, 0)), factor, 3e9))
    parts = order.step(*[x for part in parts for x in part])
    basis_next, own = newton_schulz_power(layers, *parts)
    order.through(own)
    other = over_core(own)
    (pair,) = order.step(pair)
    weights_next = order.through(
        update_weights(weights, turned, (pair, pair), ((1, 0), (2, 1)), factor, 8e9, (weights_next,))
    )
    basis_next = put_layer(*order.step(other, basis_next))
    return (weights_next, basis_next, moment_one, moment_two)


def solution(mesh):
    line = mesh.shape["shard"] == 4 and mesh.shape["tensor"] == 4

    def body(grads, *others):
        return (line_body if line and grads.shape[1] == 2 else general_body)(grads, *others)

    return jax.shard_map(
        body,
        mesh=mesh,
        in_specs=(
            P("shard", "section", "tensor", None),
            P("section", "tensor", None),
            P("section", None, None),
            P("section", ("tensor", "shard"), None),
            P("section", ("tensor", "shard"), None),
        ),
        out_specs=(
            P("section", "tensor", None),
            P("section", None, None),
            P("section", ("tensor", "shard"), None),
            P("section", ("tensor", "shard"), None),
        ),
        check_vma=False,
    )
```

```python
import functools

import jax
import jax.numpy as jnp
from jax import lax
from jax.experimental import pallas as pl
from jax.experimental.pallas import tpu as pltpu
from jax.sharding import PartitionSpec as P

NS_ITERS = 3
STEP = 1000


learn_rate = 0.5
galore_scale = 0.25
beta_one = 0.9
beta_two = 0.999
adam_eps = 1e-08
norm_eps = 1e-07
coeff_a = 3.4445
coeff_b = -4.775
coeff_c = 2.0315
highest = lax.Precision.HIGHEST


def newton_step(iterate, gram_matrix):
    squared = jnp.einsum("lrs,lst->lrt", gram_matrix, gram_matrix, precision=highest)
    mixing = coeff_b * gram_matrix + coeff_c * squared
    return coeff_a * iterate + jnp.einsum("ldr,lrs->lds", iterate, mixing, precision=highest)


def adam_direction(reduced, first_moment, second_moment):
    moment_one = beta_one * first_moment + (1.0 - beta_one) * reduced
    moment_two = beta_two * second_moment + (1.0 - beta_two) * reduced * reduced
    corrected_one = moment_one / (1.0 - beta_one**STEP)
    corrected_two = moment_two / (1.0 - beta_two**STEP)
    return (moment_one, moment_two, corrected_one / (jnp.sqrt(corrected_two) + adam_eps))


def newton_schulz(power, width):
    norms = jnp.sqrt(jnp.sum(power * power, axis=(1, 2)))
    iterate = power / (norms + norm_eps)[:, None, None]
    for sweep in range(NS_ITERS):
        gram_matrix = jnp.einsum("ldr,lds->lrs", iterate, iterate, precision=highest)
        iterate = newton_step(iterate, gram_matrix)
    return width**0.5 * iterate


def general_body(grads, weights, basis, first_moment, second_moment):
    width = basis.shape[1]
    scale_factor = width ** (-0.5)
    local_grads = grads[0]
    block_rows = first_moment.shape[1]
    summed = lax.psum_scatter(
        local_grads.astype(jnp.float32), "shard", scatter_dimension=1, tiled=True
    )
    projected = jnp.einsum("lfd,ldr->lfr", summed, basis, precision=highest)
    power = jnp.einsum("lfd,lfr->ldr", summed, projected, precision=highest)
    reduced = scale_factor * projected
    moment_one, moment_two, direction = adam_direction(reduced, first_moment, second_moment)
    factor = learn_rate * galore_scale * scale_factor
    own_start = lax.axis_index("shard") * block_rows
    current = lax.dynamic_slice_in_dim(weights, own_start, block_rows, 1)
    update = jnp.einsum("lfr,ldr->lfd", direction, basis, precision=highest)
    fresh_rows = (current.astype(jnp.float32) - factor * update).astype(jnp.bfloat16)
    weights_next = lax.all_gather(fresh_rows, "shard", axis=1, tiled=True)
    whole = lax.psum(power, ("shard", "tensor"))
    basis_next = newton_schulz(whole, width)
    return (weights_next, basis_next, moment_one, moment_two)


PLAIN = ((1,), (0,))
BOTH_LAST = ((1,), (1,))


class Place:
    def __init__(self):
        tensor, self.z = lax.axis_index("tensor"), lax.axis_index("shard")
        self.core, self.y = lax.rem(tensor, 2), lax.div(tensor, 2)
        self.inner = lax.div(lax.rem(self.z + 1, 4), 2)

    def keeps(self, j):
        return jnp.where(self.inner == 1, 1 + j, 3 * j)

    def gives(self, j):
        return jnp.where(self.inner == 1, 3 * j, 1 + j)

    def layer(self, turn):
        return self.core if turn else 1 - self.core

    def piece(self, h, k, piece):
        return pl.multiple_of((h * 4 + (self.y ^ (k // 2)) * 2 + (self.inner ^ (k % 2))) * piece, piece)


def split(x):
    high = x.astype(jnp.bfloat16)
    return high, (x - high.astype(jnp.float32)).astype(jnp.bfloat16)


def dot3(a, b, dims=PLAIN):
    dot = lambda p, q: lax.dot_general(p, q, (dims, ((), ())), preferred_element_type=jnp.float32)
    return dot(a[0], b[0]) + (dot(a[0], b[1]) + dot(a[1], b[0]))


def params(megabytes):
    return pltpu.CompilerParams(vmem_limit_bytes=megabytes * 2**20)


def in_vmem(*arrays):
    return [pltpu.with_memory_space_constraint(x, pltpu.VMEM) for x in arrays]


def local_call(kernel, outs, *operands, name, scratch=(), flops=0):
    vmem = pl.BlockSpec(memory_space=pltpu.VMEM)
    return pl.pallas_call(
        kernel,
        out_shape=[pltpu.VMEM(shape, dtype) for shape, dtype in outs],
        in_specs=[vmem] * len(operands),
        out_specs=[vmem] * len(outs),
        scratch_shapes=scratch,
        compiler_params=params(12),
        cost_estimate=cost(flops),
        name=name,
    )(*in_vmem(*operands))


def cost(flops):
    return pl.CostEstimate(flops=int(flops), bytes_accessed=0, transcendentals=0) if flops else None


SPAN = 250.0


def encode(x):
    bound = jnp.max(jnp.abs(x), axis=0, keepdims=True)
    bound = (bound * 1.01 + 1e-30).astype(jnp.bfloat16).astype(jnp.float32)
    size = jnp.exp2(jnp.abs(x) * (SPAN / bound) - SPAN / 2)
    code = jnp.where(x < 0, -size, size)
    return code.astype(jnp.bfloat16), jnp.broadcast_to(bound, (16, x.shape[1])).astype(jnp.bfloat16)


def decode(code, bound):
    code, bound = code.astype(jnp.float32), bound[0:1].astype(jnp.float32)
    size = (jnp.log2(jnp.abs(code)) + SPAN / 2) * (bound / SPAN)
    return jnp.where(code < 0, -size, size)


def prepare_kernel(grads_hbm, basis_hbm, grads_ref, high_ref, low_ref, buffer, sems):
    layers = buffer.shape[0]
    copies = [pltpu.make_async_copy(basis_hbm.at[layer], buffer.at[layer], sems.at[layer]) for layer in range(layers)]
    copies += [pltpu.make_async_copy(grads_hbm.at[0, layer], grads_ref.at[0, layer], sems.at[layers + layer]) for layer in range(layers)]
    for copy in copies:
        copy.start()
    for layer in range(layers):
        copies[layer].wait()
        high_ref[layer], low_ref[layer] = split(buffer[layer])
    for copy in copies[layers:]:
        copy.wait()


def prepare(grads, basis):
    layers = basis.shape[0]
    vmem, hbm = pl.BlockSpec(memory_space=pltpu.VMEM), pl.BlockSpec(memory_space=pltpu.HBM)
    return pl.pallas_call(
        prepare_kernel,
        out_shape=[pltpu.VMEM(grads.shape, grads.dtype)] + [pltpu.VMEM(basis.shape, jnp.bfloat16)] * 2,
        in_specs=[hbm, hbm],
        out_specs=[vmem] * 3,
        scratch_shapes=[pltpu.VMEM(basis.shape, jnp.float32), pltpu.SemaphoreType.DMA((2 * layers,))],
        compiler_params=params(12),
        name="prepare",
    )(*[pltpu.with_memory_space_constraint(x, pltpu.HBM) for x in (grads, basis)])


def fetch_kernel(weights_hbm, high_ref, low_ref, weights_ref, high_t_ref, low_t_ref, sems):
    layers = weights_ref.shape[0]
    copies = [pltpu.make_async_copy(weights_hbm.at[layer], weights_ref.at[layer], sems.at[layer]) for layer in range(layers)]
    for copy in copies:
        copy.start()
    for layer in range(layers):
        for source, out in ((high_ref, high_t_ref), (low_ref, low_t_ref)):
            out[layer] = source[layer].astype(jnp.float32).T.astype(jnp.bfloat16)
    for copy in copies:
        copy.wait()


def fetch(weights, high, low):
    layers, width, rank = high.shape
    vmem = pl.BlockSpec(memory_space=pltpu.VMEM)
    return pl.pallas_call(
        fetch_kernel,
        out_shape=[pltpu.VMEM(weights.shape, weights.dtype)] + [pltpu.VMEM((layers, rank, width), jnp.bfloat16)] * 2,
        in_specs=[pl.BlockSpec(memory_space=pltpu.HBM), vmem, vmem],
        out_specs=[vmem] * 3,
        scratch_shapes=[pltpu.SemaphoreType.DMA((layers,))],
        compiler_params=params(12),
        name="fetch",
    )(pltpu.with_memory_space_constraint(weights, pltpu.HBM), *in_vmem(high, low))


def code_blocks(code_ref, parts):
    for j, part in enumerate(parts):
        rows = part.shape[0]
        row = j * (rows + 16)
        code_ref[row : row + rows], code_ref[row + rows : row + rows + 16] = encode(part)


def blocks_of(code_ref):
    rows = code_ref.shape[0] // 2 - 16
    return [decode(code_ref[j * (rows + 16) : j * (rows + 16) + rows], code_ref[j * (rows + 16) + rows : (j + 1) * (rows + 16)]) for j in range(2)]


def rows_of(grads_ref, layer, block, rows):
    return grads_ref[0, layer, pl.ds(pl.multiple_of(block * rows, rows), rows)]


def exact_dot(a, b, dims=PLAIN):
    dot = lambda p, q: lax.dot_general(p, q, (dims, ((), ())), preferred_element_type=jnp.float32)
    return dot(a[0], b) + dot(a[1], b) if isinstance(a, tuple) else dot(a, b[0]) + dot(a, b[1])


def give_kernel(grads_hbm, basis_hbm, code_ref, blocks, basis_ref, sems):
    place = Place()
    layer, rows = place.layer(0), blocks.shape[1]
    copies = [pltpu.make_async_copy(basis_hbm.at[layer], basis_ref, sems.at[2])]
    for j in range(2):
        source = grads_hbm.at[0, layer, pl.ds(pl.multiple_of(place.gives(j) * rows, rows), rows)]
        copies.append(pltpu.make_async_copy(source, blocks.at[j], sems.at[j]))
    for copy in copies:
        copy.start()
    copies[0].wait()
    basis = split(basis_ref[...])
    parts = []
    for j in range(2):
        copies[1 + j].wait()
        parts.append(exact_dot(blocks[j], basis))
    code_blocks(code_ref, parts)


def give(grads, basis):
    rows, (_, width, rank) = grads.shape[2] // 4, basis.shape
    vmem, hbm = pl.BlockSpec(memory_space=pltpu.VMEM), pl.BlockSpec(memory_space=pltpu.HBM)
    return pl.pallas_call(
        give_kernel,
        out_shape=pltpu.VMEM((2 * (rows + 16), rank), jnp.bfloat16),
        in_specs=[hbm, hbm],
        out_specs=vmem,
        scratch_shapes=[
            pltpu.VMEM((2, rows, width), grads.dtype),
            pltpu.VMEM((width, rank), jnp.float32),
            pltpu.SemaphoreType.DMA((3,)),
        ],
        compiler_params=params(8),
        name="give",
    )(*[pltpu.with_memory_space_constraint(x, pltpu.HBM) for x in (grads, basis)])


def project_kernel(turn, grads_ref, high_ref, low_ref, out_ref, *code_refs):
    place = Place()
    layer, rows = place.layer(turn), out_ref.shape[0] // 2
    basis = high_ref[layer], low_ref[layer]
    for code_ref in code_refs:
        code_blocks(code_ref, [exact_dot(rows_of(grads_ref, layer, place.gives(j), rows), basis) for j in range(2)])
    for j in range(2):
        out_ref[j * rows : (j + 1) * rows] = exact_dot(rows_of(grads_ref, layer, place.keeps(j), rows), basis)


def project(grads, basis, turn):
    rows, rank = grads.shape[2] // 4, basis[0].shape[2]
    outs = [((2 * rows, rank), jnp.float32)] + [((2 * (rows + 16), rank), jnp.bfloat16)] * turn
    return local_call(functools.partial(project_kernel, turn), outs, grads, *basis, name="project")


def add_coded_kernel(own_ref, received_ref, out_ref, code_ref):
    rows = own_ref.shape[0] // 2
    parts = [own_ref[j * rows : (j + 1) * rows] + block for j, block in enumerate(blocks_of(received_ref))]
    code_blocks(code_ref, parts)
    for j, part in enumerate(parts):
        out_ref[j * rows : (j + 1) * rows] = part


def add_coded(own, received):
    outs = [(own.shape, jnp.float32), (received.shape, jnp.bfloat16)]
    return local_call(add_coded_kernel, outs, own, received, name="add_coded")


HALVES = 2


def power_kernel(turn, scale, grads_ref, first_ref, second_ref, kept_ref, given_ref, *rest):
    place = Place()
    code_before = rest[2] if turn else None
    half0_ref, half1_ref, one_ref, two_ref, code_ref, product, one, two, sems = rest[3 * turn :]
    rows = first_ref.shape[1]
    sums = [kept_ref[0:rows], kept_ref[rows:]]
    layer = place.layer(turn)
    reduced = scale * jnp.where(place.z < 2, sums[0], sums[1])
    one[...], two[...], direction = adam_direction(reduced, first_ref[layer], second_ref[layer])
    copies = [pltpu.make_async_copy(x, out.at[layer], sems.at[i]) for i, (x, out) in enumerate(((one, one_ref), (two, two_ref)))]
    for copy in copies:
        copy.start()
    if turn == 0:
        code_ref[0:rows], code_ref[rows:] = encode(direction)
    else:
        code_ref[1 - layer] = code_before[...]
        code_ref[layer, 0:rows], code_ref[layer, rows:] = encode(direction)
    blocks = [place.keeps(0), place.keeps(1), place.gives(0), place.gives(1)]
    rows_in_order = jnp.concatenate([rows_of(grads_ref, layer, block, rows) for block in blocks])
    product[...] = exact_dot(split(jnp.concatenate(sums + blocks_of(given_ref)).T), rows_in_order)
    piece = product.shape[0] // (4 * HALVES)
    for h in range(HALVES):
        for k in range(4):
            (half0_ref, half1_ref)[h][pl.ds(k * piece, piece)] = product[pl.ds(place.piece(h, k, piece), piece)]
    for copy in copies:
        copy.wait()


def power_product(grads, first_moment, second_moment, kept, given, turn, scale, before=()):
    width = grads.shape[3]
    layers, rows, rank = first_moment.shape
    vmem, anywhere = pl.BlockSpec(memory_space=pltpu.VMEM), pl.BlockSpec(memory_space=pl.ANY)
    operands = in_vmem(grads, first_moment, second_moment, kept, given)
    count = len(operands)
    return pl.pallas_call(
        functools.partial(power_kernel, turn, scale),
        out_shape=[pltpu.VMEM((rank // HALVES, width), jnp.float32)] * HALVES
        + [jax.ShapeDtypeStruct(first_moment.shape, jnp.float32)] * 2
        + [pltpu.VMEM((layers, rows + 16, rank) if turn else (rows + 16, rank), jnp.bfloat16)],
        in_specs=[vmem] * count + [anywhere, anywhere, vmem][: len(before)],
        out_specs=[vmem] * HALVES + [anywhere] * 2 + [vmem],
        scratch_shapes=[pltpu.VMEM((rank, width), jnp.float32)]
        + [pltpu.VMEM((rows, rank), jnp.float32)] * 2
        + [pltpu.SemaphoreType.DMA((2,))],
        input_output_aliases={count: HALVES, count + 1: HALVES + 1} if before else {},
        compiler_params=params(12),
        cost_estimate=cost(5e9 * turn),
        name="power",
    )(*operands, *before[:2], *in_vmem(*before[2:]))


def add_split_kernel(own_ref, received_ref, keep_ref, give_ref):
    half = keep_ref.shape[0]
    keep_ref[...] = own_ref[0:half] + received_ref[0:half]
    give_ref[...] = own_ref[half:] + received_ref[half:]


def add_split(own, received, flops):
    outs = [((own.shape[0] // 2, own.shape[1]), jnp.float32)] * 2
    return local_call(add_split_kernel, outs, own, received, name="add_split", flops=flops)


def add_kernel(own_ref, received_ref, out_ref):
    out_ref[...] = own_ref[...] + received_ref[...]


def join_kernel(own_ref, received_ref, out_ref):
    half = own_ref.shape[0]
    out_ref[0:half] = own_ref[...]
    out_ref[half:] = received_ref[...]


def add(own, received, flops):
    return local_call(add_kernel, [(own.shape, jnp.float32)], own, received, name="add", flops=flops)[0]


def join(own, received):
    outs = [((2 * own.shape[0], own.shape[1]), jnp.float32)]
    return local_call(join_kernel, outs, own, received, name="join")[0]


def newton_schulz_kernel(*refs):
    place = Place()
    parts, (out_ref, result_ref, power_ref, sems) = refs[:-4], refs[-4:]
    piece = parts[0].shape[0] // 2
    for h in range(HALVES):
        for k in range(4):
            part = parts[2 * h + k // 2]
            power_ref[pl.ds(place.piece(h, k, piece), piece)] = part[pl.ds(k % 2 * piece, piece)]
    power = power_ref[...]
    rank, width = power.shape
    unscaled = split(power)
    scale = 1.0 / (jnp.sqrt(jnp.sum(power * power)) + norm_eps)
    gram = dot3(unscaled, unscaled, BOTH_LAST) * scale * scale
    ident = lax.broadcasted_iota(jnp.int32, gram.shape, 0) == lax.broadcasted_iota(jnp.int32, gram.shape, 1)
    diagonal = jnp.where(ident, coeff_a, 0.0)
    product = None
    for sweep in range(NS_ITERS - 1):
        g = split(gram)
        factor = diagonal + coeff_b * gram + coeff_c * dot3(g, g)
        f = split(factor)
        gram = dot3(split(dot3(f, g)), f)
        product = f if product is None else split(dot3(product, f))
    iterate = split(dot3(product, unscaled))
    g = split(gram)
    last = split((diagonal + coeff_b * gram + coeff_c * dot3(g, g)) * (scale * width**0.5))
    copies = []
    for i in range(width // rank):
        columns = slice(i * rank, (i + 1) * rank)
        result_ref[columns] = dot3(last, [term[:, columns] for term in iterate]).T
        copies.append(pltpu.make_async_copy(result_ref.at[columns], out_ref.at[place.core, columns], sems.at[i]))
        copies[-1].start()
    for copy in copies:
        copy.wait()


def newton_schulz_power(layers, *parts):
    rank, width = 2 * HALVES * parts[0].shape[0], parts[0].shape[1]
    vmem = pl.BlockSpec(memory_space=pltpu.VMEM)
    return pl.pallas_call(
        newton_schulz_kernel,
        out_shape=[jax.ShapeDtypeStruct((layers, width, rank), jnp.float32), pltpu.VMEM((width, rank), jnp.float32)],
        in_specs=[vmem] * len(parts),
        out_specs=[pl.BlockSpec(memory_space=pl.ANY), vmem],
        scratch_shapes=[pltpu.VMEM((rank, width), jnp.float32), pltpu.SemaphoreType.DMA((width // rank,))],
        compiler_params=params(12),
        name="newton_schulz",
    )(*in_vmem(*parts))


def put_layer_kernel(layer_ref, whole_ref, out_ref, sems):
    count = sems.shape[0]
    rows = layer_ref.shape[0] // count
    copies = []
    for i in range(count):
        part = pl.ds(i * rows, rows)
        copies.append(pltpu.make_async_copy(layer_ref.at[part], out_ref.at[1 - Place().core, part], sems.at[i]))
    for copy in copies:
        copy.start()
    for copy in copies:
        copy.wait()


def put_layer(layer, whole):
    hbm = pl.BlockSpec(memory_space=pl.ANY)
    return pl.pallas_call(
        put_layer_kernel,
        out_shape=jax.ShapeDtypeStruct(whole.shape, whole.dtype),
        in_specs=[pl.BlockSpec(memory_space=pltpu.VMEM), hbm],
        out_specs=hbm,
        scratch_shapes=[pltpu.SemaphoreType.DMA((4,))],
        input_output_aliases={1: 0},
        compiler_params=params(4),
        name="put_layer",
    )(*in_vmem(layer), whole)


def stack_kernel(a_ref, b_ref, out_ref):
    out_ref[0] = a_ref[...]
    out_ref[1] = b_ref[...]


def stack(a, b):
    return local_call(stack_kernel, [((2,) + a.shape, a.dtype)], a, b, name="stack")[0]


def update_kernel(factor, blocks, weights_ref, high_ref, low_ref, *refs):
    directions, (out_ref, buffer, sems) = refs[:2], refs[-3:]
    place = Place()
    layers, rows = weights_ref.shape[0], buffer.shape[2]
    copies = []
    for layer in range(layers):
        basis = high_ref[layer], low_ref[layer]
        for i, (direction, (k, source)) in enumerate(zip(directions, blocks)):
            where = pl.ds(pl.multiple_of((place.z ^ k) * rows, rows), rows)
            exact = decode(direction[source, layer, 0:rows], direction[source, layer, rows:])
            update = dot3(split(exact), basis)
            buffer[layer, i] = (weights_ref[layer, where].astype(jnp.float32) - factor * update).astype(buffer.dtype)
            copies.append(pltpu.make_async_copy(buffer.at[layer, i], out_ref.at[layer, where], sems.at[layer, i]))
            copies[-1].start()
    for copy in copies:
        copy.wait()


def update_weights(weights, basis, directions, blocks, factor, flops, before=()):
    layers, height, width = weights.shape
    vmem, anywhere = pl.BlockSpec(memory_space=pltpu.VMEM), pl.BlockSpec(memory_space=pl.ANY)
    operands = in_vmem(weights, *basis, *directions)
    return pl.pallas_call(
        functools.partial(update_kernel, factor, blocks),
        out_shape=jax.ShapeDtypeStruct(weights.shape, weights.dtype),
        in_specs=[vmem] * len(operands) + [anywhere] * len(before),
        out_specs=anywhere,
        scratch_shapes=[pltpu.VMEM((layers, 2, height // 4, width), weights.dtype), pltpu.SemaphoreType.DMA((layers, 2))],
        input_output_aliases={5: 0} if before else {},
        compiler_params=params(12),
        cost_estimate=cost(flops),
        name="update_weights",
    )(*operands, *before)


def xor_pairs(k):
    return [(i, i ^ k) for i in range(4)]


def over_z(x, k):
    return lax.ppermute(x, "shard", xor_pairs(k))


def over_core(x):
    return lax.ppermute(x, "tensor", xor_pairs(1))


def over_y(x):
    return lax.ppermute(x, "tensor", xor_pairs(2))


class Order:
    def __init__(self):
        self.last = None

    def step(self, *operands):
        if self.last is None:
            return operands
        return lax.optimization_barrier(tuple(operands) + (self.last,))[:-1]

    def through(self, result):
        self.last = result
        return result


def line_body(grads, weights, basis, first_moment, second_moment):
    width = basis.shape[1]
    scale_factor = width ** (-0.5)
    layers, rows = grads.shape[1], first_moment.shape[1]
    order = Order()


    def product(turn, kept, given, *before):
        *halves, one, two, code = power_product(
            grads, first_moment, second_moment, *order.step(kept, given), turn, scale_factor, before
        )
        order.through(halves[0])
        return halves, (one, two, code)

    def add_code(x, received):
        x, code = add_coded(*order.step(x, received))
        return order.through(x), code

    def scatter(over, x, received, flops=0):
        keep, give = add_split(*order.step(x, received), flops)
        return order.through(keep), over(give)

    def total(over, x, received, flops=0):
        x = order.through(add(*order.step(x, received), flops))
        return x, over(x)

    def gather(over, x, received):
        x = order.through(join(*order.step(x, received)))
        return x, over(x)

    next_z = lambda x: over_z(x, 1)
    opposite_z = lambda x: over_z(x, 3)

    code = order.through(give(grads, basis))
    received = next_z(code)
    grads, high, low = prepare(*order.step(grads, basis))
    (kept,) = project(grads, (high, low), 0)
    second, second_code = project(*order.step(grads, order.through(kept))[:1], (high, low), 1)
    order.through(second)
    weights, *turned = fetch(*order.step(weights, high, low))
    order.through(weights)
    first, code = add_code(kept, received)
    first = first, opposite_z(code)
    second, code = add_code(second, next_z(order.step(second_code)[0]))
    second = second, opposite_z(code)
    sums = []
    for pair in (first, second):
        x, code = add_code(*pair)
        sums.append((x, next_z(code)))
    gifts, before = product(0, *sums[0])
    gifts = [over_core(gift) for gift in gifts]
    parts, (moment_one, moment_two, code) = product(1, *sums[1], *before)
    parts = [scatter(over_y, part, gift, 1e9) for part, gift in zip(parts, gifts)]
    opposite = opposite_z(order.step(code)[0])
    parts = [scatter(next_z, *part) for part in parts]
    opposite, *parts[0] = order.step(opposite, *parts[0])
    first = total(opposite_z, *parts[0], 1e9)
    parts = [first, total(opposite_z, *parts[1])]
    parts = [total(next_z, *part) for part in parts]
    parts = [gather(over_y, *part) for part in parts]
    pair = next_z(order.through(stack(*order.step(code, opposite))))
    factor = learn_rate * galore_scale * scale_factor
    code, opposite, weights, *parts[0] = order.step(code[None], opposite[None], weights, *parts[0])
    weights_next = order.through(update_weights(weights, turned, (code, opposite), ((0, 0), (3, 0)), factor, 3e9))
    parts = order.step(*[x for part in parts for x in part])
    basis_next, own = newton_schulz_power(layers, *parts)
    order.through(own)
    other = over_core(own)
    (pair,) = order.step(pair)
    weights_next = order.through(
        update_weights(weights, turned, (pair, pair), ((1, 0), (2, 1)), factor, 8e9, (weights_next,))
    )
    basis_next = put_layer(*order.step(other, basis_next))
    return (weights_next, basis_next, moment_one, moment_two)


def solution(mesh):
    line = mesh.shape["shard"] == 4 and mesh.shape["tensor"] == 4

    def body(grads, *others):
        return (line_body if line and grads.shape[1] == 2 else general_body)(grads, *others)

    return jax.shard_map(
        body,
        mesh=mesh,
        in_specs=(
            P("shard", "section", "tensor", None),
            P("section", "tensor", None),
            P("section", None, None),
            P("section", ("tensor", "shard"), None),
            P("section", ("tensor", "shard"), None),
        ),
        out_specs=(
            P("section", "tensor", None),
            P("section", None, None),
            P("section", ("tensor", "shard"), None),
            P("section", ("tensor", "shard"), None),
        ),
        check_vma=False,
    )
```

```python
import functools

import jax
import jax.numpy as jnp
from jax import lax
from jax.experimental import pallas as pl
from jax.experimental.pallas import tpu as pltpu
from jax.sharding import PartitionSpec as P

NS_ITERS = 3
STEP = 1000


learn_rate = 0.5
galore_scale = 0.25
beta_one = 0.9
beta_two = 0.999
adam_eps = 1e-08
norm_eps = 1e-07
coeff_a = 3.4445
coeff_b = -4.775
coeff_c = 2.0315
highest = lax.Precision.HIGHEST


def newton_step(iterate, gram_matrix):
    squared = jnp.einsum("lrs,lst->lrt", gram_matrix, gram_matrix, precision=highest)
    mixing = coeff_b * gram_matrix + coeff_c * squared
    return coeff_a * iterate + jnp.einsum("ldr,lrs->lds", iterate, mixing, precision=highest)


def adam_direction(reduced, first_moment, second_moment):
    moment_one = beta_one * first_moment + (1.0 - beta_one) * reduced
    moment_two = beta_two * second_moment + (1.0 - beta_two) * reduced * reduced
    corrected_one = moment_one / (1.0 - beta_one**STEP)
    corrected_two = moment_two / (1.0 - beta_two**STEP)
    return (moment_one, moment_two, corrected_one / (jnp.sqrt(corrected_two) + adam_eps))


def newton_schulz(power, width):
    norms = jnp.sqrt(jnp.sum(power * power, axis=(1, 2)))
    iterate = power / (norms + norm_eps)[:, None, None]
    for sweep in range(NS_ITERS):
        gram_matrix = jnp.einsum("ldr,lds->lrs", iterate, iterate, precision=highest)
        iterate = newton_step(iterate, gram_matrix)
    return width**0.5 * iterate


def general_body(grads, weights, basis, first_moment, second_moment):
    width = basis.shape[1]
    scale_factor = width ** (-0.5)
    local_grads = grads[0]
    block_rows = first_moment.shape[1]
    summed = lax.psum_scatter(
        local_grads.astype(jnp.float32), "shard", scatter_dimension=1, tiled=True
    )
    projected = jnp.einsum("lfd,ldr->lfr", summed, basis, precision=highest)
    power = jnp.einsum("lfd,lfr->ldr", summed, projected, precision=highest)
    reduced = scale_factor * projected
    moment_one, moment_two, direction = adam_direction(reduced, first_moment, second_moment)
    factor = learn_rate * galore_scale * scale_factor
    own_start = lax.axis_index("shard") * block_rows
    current = lax.dynamic_slice_in_dim(weights, own_start, block_rows, 1)
    update = jnp.einsum("lfr,ldr->lfd", direction, basis, precision=highest)
    fresh_rows = (current.astype(jnp.float32) - factor * update).astype(jnp.bfloat16)
    weights_next = lax.all_gather(fresh_rows, "shard", axis=1, tiled=True)
    whole = lax.psum(power, ("shard", "tensor"))
    basis_next = newton_schulz(whole, width)
    return (weights_next, basis_next, moment_one, moment_two)


PLAIN = ((1,), (0,))
BOTH_LAST = ((1,), (1,))


class Place:
    def __init__(self):
        tensor, self.z = lax.axis_index("tensor"), lax.axis_index("shard")
        self.core, self.y = lax.rem(tensor, 2), lax.div(tensor, 2)
        self.inner = lax.div(lax.rem(self.z + 1, 4), 2)

    def keeps(self, j):
        return jnp.where(self.inner == 1, 1 + j, 3 * j)

    def gives(self, j):
        return jnp.where(self.inner == 1, 3 * j, 1 + j)

    def layer(self, turn):
        return self.core if turn else 1 - self.core

    def piece(self, h, k, piece):
        return pl.multiple_of((h * 4 + (self.y ^ (k // 2)) * 2 + (self.inner ^ (k % 2))) * piece, piece)


def split(x):
    high = x.astype(jnp.bfloat16)
    return high, (x - high.astype(jnp.float32)).astype(jnp.bfloat16)


def dot3(a, b, dims=PLAIN):
    dot = lambda p, q: lax.dot_general(p, q, (dims, ((), ())), preferred_element_type=jnp.float32)
    return dot(a[0], b[0]) + (dot(a[0], b[1]) + dot(a[1], b[0]))


def params(megabytes):
    return pltpu.CompilerParams(vmem_limit_bytes=megabytes * 2**20)


def in_vmem(*arrays):
    return [pltpu.with_memory_space_constraint(x, pltpu.VMEM) for x in arrays]


def local_call(kernel, outs, *operands, name, scratch=(), flops=0):
    vmem = pl.BlockSpec(memory_space=pltpu.VMEM)
    return pl.pallas_call(
        kernel,
        out_shape=[pltpu.VMEM(shape, dtype) for shape, dtype in outs],
        in_specs=[vmem] * len(operands),
        out_specs=[vmem] * len(outs),
        scratch_shapes=scratch,
        compiler_params=params(12),
        cost_estimate=cost(flops),
        name=name,
    )(*in_vmem(*operands))


def cost(flops):
    return pl.CostEstimate(flops=int(flops), bytes_accessed=0, transcendentals=0) if flops else None


SPAN = 250.0


def encode(x):
    bound = jnp.max(jnp.abs(x), axis=0, keepdims=True)
    bound = (bound * 1.01 + 1e-30).astype(jnp.bfloat16).astype(jnp.float32)
    size = jnp.exp2(jnp.abs(x) * (SPAN / bound) - SPAN / 2)
    code = jnp.where(x < 0, -size, size)
    return code.astype(jnp.bfloat16), jnp.broadcast_to(bound, (16, x.shape[1])).astype(jnp.bfloat16)


def decode(code, bound):
    code, bound = code.astype(jnp.float32), bound[0:1].astype(jnp.float32)
    size = (jnp.log2(jnp.abs(code)) + SPAN / 2) * (bound / SPAN)
    return jnp.where(code < 0, -size, size)


def prepare_kernel(grads_hbm, basis_hbm, grads_ref, high_ref, low_ref, buffer, sems):
    layers = buffer.shape[0]
    copies = [pltpu.make_async_copy(basis_hbm.at[layer], buffer.at[layer], sems.at[layer]) for layer in range(layers)]
    copies += [pltpu.make_async_copy(grads_hbm.at[0, layer], grads_ref.at[0, layer], sems.at[layers + layer]) for layer in range(layers)]
    for copy in copies:
        copy.start()
    for layer in range(layers):
        copies[layer].wait()
        high_ref[layer], low_ref[layer] = split(buffer[layer])
    for copy in copies[layers:]:
        copy.wait()


def prepare(grads, basis):
    layers = basis.shape[0]
    vmem, hbm = pl.BlockSpec(memory_space=pltpu.VMEM), pl.BlockSpec(memory_space=pltpu.HBM)
    return pl.pallas_call(
        prepare_kernel,
        out_shape=[pltpu.VMEM(grads.shape, grads.dtype)] + [pltpu.VMEM(basis.shape, jnp.bfloat16)] * 2,
        in_specs=[hbm, hbm],
        out_specs=[vmem] * 3,
        scratch_shapes=[pltpu.VMEM(basis.shape, jnp.float32), pltpu.SemaphoreType.DMA((2 * layers,))],
        compiler_params=params(12),
        name="prepare",
    )(*[pltpu.with_memory_space_constraint(x, pltpu.HBM) for x in (grads, basis)])


def fetch_kernel(weights_hbm, high_ref, low_ref, weights_ref, high_t_ref, low_t_ref, sems):
    layers = weights_ref.shape[0]
    copies = [pltpu.make_async_copy(weights_hbm.at[layer], weights_ref.at[layer], sems.at[layer]) for layer in range(layers)]
    for copy in copies:
        copy.start()
    for layer in range(layers):
        for source, out in ((high_ref, high_t_ref), (low_ref, low_t_ref)):
            out[layer] = source[layer].astype(jnp.float32).T.astype(jnp.bfloat16)
    for copy in copies:
        copy.wait()


def fetch(weights, high, low):
    layers, width, rank = high.shape
    vmem = pl.BlockSpec(memory_space=pltpu.VMEM)
    return pl.pallas_call(
        fetch_kernel,
        out_shape=[pltpu.VMEM(weights.shape, weights.dtype)] + [pltpu.VMEM((layers, rank, width), jnp.bfloat16)] * 2,
        in_specs=[pl.BlockSpec(memory_space=pltpu.HBM), vmem, vmem],
        out_specs=[vmem] * 3,
        scratch_shapes=[pltpu.SemaphoreType.DMA((layers,))],
        compiler_params=params(12),
        name="fetch",
    )(pltpu.with_memory_space_constraint(weights, pltpu.HBM), *in_vmem(high, low))


def code_blocks(code_ref, parts):
    for j, part in enumerate(parts):
        rows = part.shape[0]
        row = j * (rows + 16)
        code_ref[row : row + rows], code_ref[row + rows : row + rows + 16] = encode(part)


def blocks_of(code_ref):
    rows = code_ref.shape[0] // 2 - 16
    return [decode(code_ref[j * (rows + 16) : j * (rows + 16) + rows], code_ref[j * (rows + 16) + rows : (j + 1) * (rows + 16)]) for j in range(2)]


def rows_of(grads_ref, layer, block, rows):
    return grads_ref[0, layer, pl.ds(pl.multiple_of(block * rows, rows), rows)]


def exact_dot(a, b, dims=PLAIN):
    dot = lambda p, q: lax.dot_general(p, q, (dims, ((), ())), preferred_element_type=jnp.float32)
    return dot(a[0], b) + dot(a[1], b) if isinstance(a, tuple) else dot(a, b[0]) + dot(a, b[1])


def give_kernel(grads_hbm, basis_hbm, code_ref, blocks, basis_ref, sems):
    place = Place()
    layer, rows = place.layer(0), blocks.shape[1]
    copies = [pltpu.make_async_copy(basis_hbm.at[layer], basis_ref, sems.at[2])]
    for j in range(2):
        source = grads_hbm.at[0, layer, pl.ds(pl.multiple_of(place.gives(j) * rows, rows), rows)]
        copies.append(pltpu.make_async_copy(source, blocks.at[j], sems.at[j]))
    for copy in copies:
        copy.start()
    copies[0].wait()
    basis = split(basis_ref[...])
    parts = []
    for j in range(2):
        copies[1 + j].wait()
        parts.append(exact_dot(blocks[j], basis))
    code_blocks(code_ref, parts)


def give(grads, basis):
    rows, (_, width, rank) = grads.shape[2] // 4, basis.shape
    vmem, hbm = pl.BlockSpec(memory_space=pltpu.VMEM), pl.BlockSpec(memory_space=pltpu.HBM)
    return pl.pallas_call(
        give_kernel,
        out_shape=pltpu.VMEM((2 * (rows + 16), rank), jnp.bfloat16),
        in_specs=[hbm, hbm],
        out_specs=vmem,
        scratch_shapes=[
            pltpu.VMEM((2, rows, width), grads.dtype),
            pltpu.VMEM((width, rank), jnp.float32),
            pltpu.SemaphoreType.DMA((3,)),
        ],
        compiler_params=params(8),
        name="give",
    )(*[pltpu.with_memory_space_constraint(x, pltpu.HBM) for x in (grads, basis)])


def project_kernel(turn, grads_ref, high_ref, low_ref, out_ref, *code_refs):
    place = Place()
    layer, rows = place.layer(turn), out_ref.shape[0] // 2
    basis = high_ref[layer], low_ref[layer]
    for code_ref in code_refs:
        code_blocks(code_ref, [exact_dot(rows_of(grads_ref, layer, place.gives(j), rows), basis) for j in range(2)])
    for j in range(2):
        out_ref[j * rows : (j + 1) * rows] = exact_dot(rows_of(grads_ref, layer, place.keeps(j), rows), basis)


def project(grads, basis, turn):
    rows, rank = grads.shape[2] // 4, basis[0].shape[2]
    outs = [((2 * rows, rank), jnp.float32)] + [((2 * (rows + 16), rank), jnp.bfloat16)] * turn
    return local_call(functools.partial(project_kernel, turn), outs, grads, *basis, name="project")


def add_coded_kernel(own_ref, received_ref, out_ref, code_ref):
    rows = own_ref.shape[0] // 2
    parts = [own_ref[j * rows : (j + 1) * rows] + block for j, block in enumerate(blocks_of(received_ref))]
    code_blocks(code_ref, parts)
    for j, part in enumerate(parts):
        out_ref[j * rows : (j + 1) * rows] = part


def add_coded(own, received):
    outs = [(own.shape, jnp.float32), (received.shape, jnp.bfloat16)]
    return local_call(add_coded_kernel, outs, own, received, name="add_coded")


HALVES = 2


def power_kernel(turn, scale, grads_ref, first_ref, second_ref, kept_ref, given_ref, *rest):
    place = Place()
    code_before = rest[2] if turn else None
    half0_ref, half1_ref, one_ref, two_ref, code_ref, product, one, two, sems = rest[3 * turn :]
    rows = first_ref.shape[1]
    sums = [kept_ref[0:rows], kept_ref[rows:]]
    layer = place.layer(turn)
    reduced = scale * jnp.where(place.z < 2, sums[0], sums[1])
    one[...], two[...], direction = adam_direction(reduced, first_ref[layer], second_ref[layer])
    copies = [pltpu.make_async_copy(x, out.at[layer], sems.at[i]) for i, (x, out) in enumerate(((one, one_ref), (two, two_ref)))]
    for copy in copies:
        copy.start()
    if turn == 0:
        code_ref[0:rows], code_ref[rows:] = encode(direction)
    else:
        code_ref[1 - layer] = code_before[...]
        code_ref[layer, 0:rows], code_ref[layer, rows:] = encode(direction)
    blocks = [place.keeps(0), place.keeps(1), place.gives(0), place.gives(1)]
    rows_in_order = jnp.concatenate([rows_of(grads_ref, layer, block, rows) for block in blocks])
    product[...] = exact_dot(split(jnp.concatenate(sums + blocks_of(given_ref)).T), rows_in_order)
    piece = product.shape[0] // (4 * HALVES)
    for h in range(HALVES):
        for k in range(4):
            (half0_ref, half1_ref)[h][pl.ds(k * piece, piece)] = product[pl.ds(place.piece(h, k, piece), piece)]
    for copy in copies:
        copy.wait()


def power_product(grads, first_moment, second_moment, kept, given, turn, scale, before=()):
    width = grads.shape[3]
    layers, rows, rank = first_moment.shape
    vmem, anywhere = pl.BlockSpec(memory_space=pltpu.VMEM), pl.BlockSpec(memory_space=pl.ANY)
    operands = in_vmem(grads, first_moment, second_moment, kept, given)
    count = len(operands)
    return pl.pallas_call(
        functools.partial(power_kernel, turn, scale),
        out_shape=[pltpu.VMEM((rank // HALVES, width), jnp.float32)] * HALVES
        + [jax.ShapeDtypeStruct(first_moment.shape, jnp.float32)] * 2
        + [pltpu.VMEM((layers, rows + 16, rank) if turn else (rows + 16, rank), jnp.bfloat16)],
        in_specs=[vmem] * count + [anywhere, anywhere, vmem][: len(before)],
        out_specs=[vmem] * HALVES + [anywhere] * 2 + [vmem],
        scratch_shapes=[pltpu.VMEM((rank, width), jnp.float32)]
        + [pltpu.VMEM((rows, rank), jnp.float32)] * 2
        + [pltpu.SemaphoreType.DMA((2,))],
        input_output_aliases={count: HALVES, count + 1: HALVES + 1} if before else {},
        compiler_params=params(12),
        cost_estimate=cost(5e9 * turn),
        name="power",
    )(*operands, *before[:2], *in_vmem(*before[2:]))


def add_split_kernel(own_ref, received_ref, keep_ref, give_ref):
    half = keep_ref.shape[0]
    keep_ref[...] = own_ref[0:half] + received_ref[0:half]
    give_ref[...] = own_ref[half:] + received_ref[half:]


def add_split(own, received, flops):
    outs = [((own.shape[0] // 2, own.shape[1]), jnp.float32)] * 2
    return local_call(add_split_kernel, outs, own, received, name="add_split", flops=flops)


def add_kernel(own_ref, received_ref, out_ref):
    out_ref[...] = own_ref[...] + received_ref[...]


def join_kernel(own_ref, received_ref, out_ref):
    half = own_ref.shape[0]
    out_ref[0:half] = own_ref[...]
    out_ref[half:] = received_ref[...]


def add(own, received, flops):
    return local_call(add_kernel, [(own.shape, jnp.float32)], own, received, name="add", flops=flops)[0]


def join(own, received):
    outs = [((2 * own.shape[0], own.shape[1]), jnp.float32)]
    return local_call(join_kernel, outs, own, received, name="join")[0]


def newton_schulz_kernel(*refs):
    place = Place()
    parts, (result_ref, power_ref) = refs[:-2], refs[-2:]
    piece = parts[0].shape[0] // 2
    for h in range(HALVES):
        for k in range(4):
            part = parts[2 * h + k // 2]
            power_ref[pl.ds(place.piece(h, k, piece), piece)] = part[pl.ds(k % 2 * piece, piece)]
    power = power_ref[...]
    rank, width = power.shape
    unscaled = split(power)
    scale = 1.0 / (jnp.sqrt(jnp.sum(power * power)) + norm_eps)
    gram = dot3(unscaled, unscaled, BOTH_LAST) * scale * scale
    ident = lax.broadcasted_iota(jnp.int32, gram.shape, 0) == lax.broadcasted_iota(jnp.int32, gram.shape, 1)
    diagonal = jnp.where(ident, coeff_a, 0.0)
    product = None
    for sweep in range(NS_ITERS - 1):
        g = split(gram)
        factor = diagonal + coeff_b * gram + coeff_c * dot3(g, g)
        f = split(factor)
        gram = dot3(split(dot3(f, g)), f)
        product = f if product is None else split(dot3(product, f))
    iterate = split(dot3(product, unscaled))
    g = split(gram)
    last = split((diagonal + coeff_b * gram + coeff_c * dot3(g, g)) * (scale * width**0.5))
    for i in range(width // rank):
        columns = slice(i * rank, (i + 1) * rank)
        result_ref[columns] = dot3(last, [term[:, columns] for term in iterate]).T


def newton_schulz_power(*parts):
    rank, width = 2 * HALVES * parts[0].shape[0], parts[0].shape[1]
    scratch = [pltpu.VMEM((rank, width), jnp.float32)]
    return local_call(newton_schulz_kernel, [((width, rank), jnp.float32)], *parts, name="newton_schulz", scratch=scratch)[0]


def put_layer_kernel(layer_ref, whole_ref, out_ref, sems):
    count = sems.shape[0]
    rows = layer_ref.shape[0] // count
    copies = []
    for i in range(count):
        part = pl.ds(i * rows, rows)
        copies.append(pltpu.make_async_copy(layer_ref.at[part], out_ref.at[1 - Place().core, part], sems.at[i]))
    for copy in copies:
        copy.start()
    for copy in copies:
        copy.wait()


def put_layer(layer, whole):
    hbm = pl.BlockSpec(memory_space=pl.ANY)
    return pl.pallas_call(
        put_layer_kernel,
        out_shape=jax.ShapeDtypeStruct(whole.shape, whole.dtype),
        in_specs=[pl.BlockSpec(memory_space=pltpu.VMEM), hbm],
        out_specs=hbm,
        scratch_shapes=[pltpu.SemaphoreType.DMA((4,))],
        input_output_aliases={1: 0},
        compiler_params=params(4),
        name="put_layer",
    )(*in_vmem(layer), whole)


def stack_kernel(a_ref, b_ref, out_ref):
    out_ref[0] = a_ref[...]
    out_ref[1] = b_ref[...]


def stack(a, b):
    return local_call(stack_kernel, [((2,) + a.shape, a.dtype)], a, b, name="stack")[0]


def update_kernel(factor, blocks, weights_ref, high_ref, low_ref, *refs):
    directions, (buffer, sems) = refs[:2], refs[-2:]
    place = Place()
    layers, rows = weights_ref.shape[0], buffer.shape[2]
    copies = []
    if len(refs) == 5:
        out_ref = refs[2]
    else:
        own_ref, _, out_ref, basis_ref = refs[2:6]
        copies.append(pltpu.make_async_copy(own_ref, basis_ref.at[place.core], sems.at[layers, 0]))
        copies[0].start()
    for layer in range(layers):
        basis = high_ref[layer], low_ref[layer]
        for i, (direction, (k, source)) in enumerate(zip(directions, blocks)):
            where = pl.ds(pl.multiple_of((place.z ^ k) * rows, rows), rows)
            exact = decode(direction[source, layer, 0:rows], direction[source, layer, rows:])
            update = dot3(split(exact), basis)
            buffer[layer, i] = (weights_ref[layer, where].astype(jnp.float32) - factor * update).astype(buffer.dtype)
            copies.append(pltpu.make_async_copy(buffer.at[layer, i], out_ref.at[layer, where], sems.at[layer, i]))
            copies[-1].start()
    for copy in copies:
        copy.wait()


def update_weights(weights, basis, directions, blocks, factor, flops, own=None, before=None):
    layers, height, width = weights.shape
    vmem, anywhere = pl.BlockSpec(memory_space=pltpu.VMEM), pl.BlockSpec(memory_space=pl.ANY)
    last = before is not None
    operands = in_vmem(weights, *basis, *directions, *([own] if last else []))
    outs = [jax.ShapeDtypeStruct(weights.shape, weights.dtype)]
    if last:
        outs.append(jax.ShapeDtypeStruct((layers,) + own.shape, own.dtype))
    return pl.pallas_call(
        functools.partial(update_kernel, factor, blocks),
        out_shape=outs,
        in_specs=[vmem] * len(operands) + [anywhere] * last,
        out_specs=[anywhere] * len(outs),
        scratch_shapes=[pltpu.VMEM((layers, 2, height // 4, width), weights.dtype), pltpu.SemaphoreType.DMA((layers + 1, 2))],
        input_output_aliases={6: 0} if last else {},
        compiler_params=params(12),
        cost_estimate=cost(flops),
        name="update_weights",
    )(*operands, *([before] if last else []))


def xor_pairs(k):
    return [(i, i ^ k) for i in range(4)]


def over_z(x, k):
    return lax.ppermute(x, "shard", xor_pairs(k))


def over_core(x):
    return lax.ppermute(x, "tensor", xor_pairs(1))


def over_y(x):
    return lax.ppermute(x, "tensor", xor_pairs(2))


class Order:
    def __init__(self):
        self.last = None

    def step(self, *operands):
        if self.last is None:
            return operands
        return lax.optimization_barrier(tuple(operands) + (self.last,))[:-1]

    def through(self, result):
        self.last = result
        return result


def line_body(grads, weights, basis, first_moment, second_moment):
    width = basis.shape[1]
    scale_factor = width ** (-0.5)
    layers, rows = grads.shape[1], first_moment.shape[1]
    order = Order()


    def product(turn, kept, given, *before):
        *halves, one, two, code = power_product(
            grads, first_moment, second_moment, *order.step(kept, given), turn, scale_factor, before
        )
        order.through(halves[0])
        return halves, (one, two, code)

    def add_code(x, received):
        x, code = add_coded(*order.step(x, received))
        return order.through(x), code

    def scatter(over, x, received, flops=0):
        keep, give = add_split(*order.step(x, received), flops)
        return order.through(keep), over(give)

    def total(over, x, received, flops=0):
        x = order.through(add(*order.step(x, received), flops))
        return x, over(x)

    def gather(over, x, received):
        x = order.through(join(*order.step(x, received)))
        return x, over(x)

    next_z = lambda x: over_z(x, 1)
    opposite_z = lambda x: over_z(x, 3)

    code = order.through(give(grads, basis))
    received = next_z(code)
    grads, high, low = prepare(*order.step(grads, basis))
    (kept,) = project(grads, (high, low), 0)
    second, second_code = project(*order.step(grads, order.through(kept))[:1], (high, low), 1)
    order.through(second)
    weights, *turned = fetch(*order.step(weights, high, low))
    order.through(weights)
    first, code = add_code(kept, received)
    first = first, opposite_z(code)
    second, code = add_code(second, next_z(order.step(second_code)[0]))
    second = second, opposite_z(code)
    sums = []
    for pair in (first, second):
        x, code = add_code(*pair)
        sums.append((x, next_z(code)))
    gifts, before = product(0, *sums[0])
    gifts = [over_core(gift) for gift in gifts]
    parts, (moment_one, moment_two, code) = product(1, *sums[1], *before)
    parts = [scatter(over_y, part, gift, 1e9) for part, gift in zip(parts, gifts)]
    opposite = opposite_z(order.step(code)[0])
    parts = [scatter(next_z, *part) for part in parts]
    opposite, *parts[0] = order.step(opposite, *parts[0])
    first = total(opposite_z, *parts[0], 1e9)
    parts = [first, total(opposite_z, *parts[1])]
    parts = [total(next_z, *part) for part in parts]
    parts = [gather(over_y, *part) for part in parts]
    pair = next_z(order.through(stack(*order.step(code, opposite))))
    factor = learn_rate * galore_scale * scale_factor
    code, opposite, weights, *parts[0] = order.step(code[None], opposite[None], weights, *parts[0])
    (weights_next,) = update_weights(weights, turned, (code, opposite), ((0, 0), (3, 0)), factor, 3e9)
    order.through(weights_next)
    parts = order.step(*[x for part in parts for x in part])
    own = newton_schulz_power(*parts)
    order.through(own)
    other = over_core(own)
    (pair,) = order.step(pair)
    weights_next, basis_next = update_weights(weights, turned, (pair, pair), ((1, 0), (2, 1)), factor, 8e9, own, weights_next)
    order.through(weights_next)
    basis_next = put_layer(*order.step(other, basis_next))
    return (weights_next, basis_next, moment_one, moment_two)


def solution(mesh):
    line = mesh.shape["shard"] == 4 and mesh.shape["tensor"] == 4

    def body(grads, *others):
        return (line_body if line and grads.shape[1] == 2 else general_body)(grads, *others)

    return jax.shard_map(
        body,
        mesh=mesh,
        in_specs=(
            P("shard", "section", "tensor", None),
            P("section", "tensor", None),
            P("section", None, None),
            P("section", ("tensor", "shard"), None),
            P("section", ("tensor", "shard"), None),
        ),
        out_specs=(
            P("section", "tensor", None),
            P("section", None, None),
            P("section", ("tensor", "shard"), None),
            P("section", ("tensor", "shard"), None),
        ),
        check_vma=False,
    )
```

```python
import functools

import jax
import jax.numpy as jnp
from jax import lax
from jax.experimental import pallas as pl
from jax.experimental.pallas import tpu as pltpu
from jax.sharding import PartitionSpec as P

NS_ITERS = 3
STEP = 1000


learn_rate = 0.5
galore_scale = 0.25
beta_one = 0.9
beta_two = 0.999
adam_eps = 1e-08
norm_eps = 1e-07
coeff_a = 3.4445
coeff_b = -4.775
coeff_c = 2.0315
highest = lax.Precision.HIGHEST


def newton_step(iterate, gram_matrix):
    squared = jnp.einsum("lrs,lst->lrt", gram_matrix, gram_matrix, precision=highest)
    mixing = coeff_b * gram_matrix + coeff_c * squared
    return coeff_a * iterate + jnp.einsum("ldr,lrs->lds", iterate, mixing, precision=highest)


def adam_direction(reduced, first_moment, second_moment):
    moment_one = beta_one * first_moment + (1.0 - beta_one) * reduced
    moment_two = beta_two * second_moment + (1.0 - beta_two) * reduced * reduced
    corrected_one = moment_one / (1.0 - beta_one**STEP)
    corrected_two = moment_two / (1.0 - beta_two**STEP)
    return (moment_one, moment_two, corrected_one / (jnp.sqrt(corrected_two) + adam_eps))


def newton_schulz(power, width):
    norms = jnp.sqrt(jnp.sum(power * power, axis=(1, 2)))
    iterate = power / (norms + norm_eps)[:, None, None]
    for sweep in range(NS_ITERS):
        gram_matrix = jnp.einsum("ldr,lds->lrs", iterate, iterate, precision=highest)
        iterate = newton_step(iterate, gram_matrix)
    return width**0.5 * iterate


def general_body(grads, weights, basis, first_moment, second_moment):
    width = basis.shape[1]
    scale_factor = width ** (-0.5)
    local_grads = grads[0]
    block_rows = first_moment.shape[1]
    summed = lax.psum_scatter(
        local_grads.astype(jnp.float32), "shard", scatter_dimension=1, tiled=True
    )
    projected = jnp.einsum("lfd,ldr->lfr", summed, basis, precision=highest)
    power = jnp.einsum("lfd,lfr->ldr", summed, projected, precision=highest)
    reduced = scale_factor * projected
    moment_one, moment_two, direction = adam_direction(reduced, first_moment, second_moment)
    factor = learn_rate * galore_scale * scale_factor
    own_start = lax.axis_index("shard") * block_rows
    current = lax.dynamic_slice_in_dim(weights, own_start, block_rows, 1)
    update = jnp.einsum("lfr,ldr->lfd", direction, basis, precision=highest)
    fresh_rows = (current.astype(jnp.float32) - factor * update).astype(jnp.bfloat16)
    weights_next = lax.all_gather(fresh_rows, "shard", axis=1, tiled=True)
    whole = lax.psum(power, ("shard", "tensor"))
    basis_next = newton_schulz(whole, width)
    return (weights_next, basis_next, moment_one, moment_two)


PLAIN = ((1,), (0,))
BOTH_LAST = ((1,), (1,))


class Place:
    def __init__(self):
        tensor, self.z = lax.axis_index("tensor"), lax.axis_index("shard")
        self.core, self.y = lax.rem(tensor, 2), lax.div(tensor, 2)
        self.inner = lax.div(lax.rem(self.z + 1, 4), 2)

    def keeps(self, j):
        return jnp.where(self.inner == 1, 1 + j, 3 * j)

    def gives(self, j):
        return jnp.where(self.inner == 1, 3 * j, 1 + j)

    def layer(self, turn):
        return self.core if turn else 1 - self.core

    def piece(self, h, k, piece):
        return pl.multiple_of((h * 4 + (self.y ^ (k // 2)) * 2 + (self.inner ^ (k % 2))) * piece, piece)


def split(x):
    high = x.astype(jnp.bfloat16)
    return high, (x - high.astype(jnp.float32)).astype(jnp.bfloat16)


def dot3(a, b, dims=PLAIN):
    dot = lambda p, q: lax.dot_general(p, q, (dims, ((), ())), preferred_element_type=jnp.float32)
    return dot(a[0], b[0]) + (dot(a[0], b[1]) + dot(a[1], b[0]))


def params(megabytes):
    return pltpu.CompilerParams(vmem_limit_bytes=megabytes * 2**20)


def in_vmem(*arrays):
    return [pltpu.with_memory_space_constraint(x, pltpu.VMEM) for x in arrays]


def local_call(kernel, outs, *operands, name, scratch=(), flops=0):
    vmem = pl.BlockSpec(memory_space=pltpu.VMEM)
    return pl.pallas_call(
        kernel,
        out_shape=[pltpu.VMEM(shape, dtype) for shape, dtype in outs],
        in_specs=[vmem] * len(operands),
        out_specs=[vmem] * len(outs),
        scratch_shapes=scratch,
        compiler_params=params(12),
        cost_estimate=cost(flops),
        name=name,
    )(*in_vmem(*operands))


def cost(flops):
    return pl.CostEstimate(flops=int(flops), bytes_accessed=0, transcendentals=0) if flops else None


SPAN = 250.0


def encode(x):
    bound = jnp.max(jnp.abs(x), axis=0, keepdims=True)
    bound = (bound * 1.01 + 1e-30).astype(jnp.bfloat16).astype(jnp.float32)
    size = jnp.exp2(jnp.abs(x) * (SPAN / bound) - SPAN / 2)
    code = jnp.where(x < 0, -size, size)
    return code.astype(jnp.bfloat16), jnp.broadcast_to(bound, (16, x.shape[1])).astype(jnp.bfloat16)


def decode(code, bound):
    code, bound = code.astype(jnp.float32), bound[0:1].astype(jnp.float32)
    size = (jnp.log2(jnp.abs(code)) + SPAN / 2) * (bound / SPAN)
    return jnp.where(code < 0, -size, size)


def prepare_kernel(grads_hbm, basis_hbm, grads_ref, high_ref, low_ref, buffer, sems):
    layers = buffer.shape[0]
    copies = [pltpu.make_async_copy(basis_hbm.at[layer], buffer.at[layer], sems.at[layer]) for layer in range(layers)]
    copies += [pltpu.make_async_copy(grads_hbm.at[0, layer], grads_ref.at[0, layer], sems.at[layers + layer]) for layer in range(layers)]
    for copy in copies:
        copy.start()
    for layer in range(layers):
        copies[layer].wait()
        high_ref[layer], low_ref[layer] = split(buffer[layer])
    for copy in copies[layers:]:
        copy.wait()


def prepare(grads, basis):
    layers = basis.shape[0]
    vmem, hbm = pl.BlockSpec(memory_space=pltpu.VMEM), pl.BlockSpec(memory_space=pltpu.HBM)
    return pl.pallas_call(
        prepare_kernel,
        out_shape=[pltpu.VMEM(grads.shape, grads.dtype)] + [pltpu.VMEM(basis.shape, jnp.bfloat16)] * 2,
        in_specs=[hbm, hbm],
        out_specs=[vmem] * 3,
        scratch_shapes=[pltpu.VMEM(basis.shape, jnp.float32), pltpu.SemaphoreType.DMA((2 * layers,))],
        compiler_params=params(12),
        name="prepare",
    )(*[pltpu.with_memory_space_constraint(x, pltpu.HBM) for x in (grads, basis)])


def fetch_kernel(weights_hbm, high_ref, low_ref, weights_ref, high_t_ref, low_t_ref, sems):
    layers = weights_ref.shape[0]
    copies = [pltpu.make_async_copy(weights_hbm.at[layer], weights_ref.at[layer], sems.at[layer]) for layer in range(layers)]
    for copy in copies:
        copy.start()
    for layer in range(layers):
        for source, out in ((high_ref, high_t_ref), (low_ref, low_t_ref)):
            out[layer] = source[layer].astype(jnp.float32).T.astype(jnp.bfloat16)
    for copy in copies:
        copy.wait()


def fetch(weights, high, low):
    layers, width, rank = high.shape
    vmem = pl.BlockSpec(memory_space=pltpu.VMEM)
    return pl.pallas_call(
        fetch_kernel,
        out_shape=[pltpu.VMEM(weights.shape, weights.dtype)] + [pltpu.VMEM((layers, rank, width), jnp.bfloat16)] * 2,
        in_specs=[pl.BlockSpec(memory_space=pltpu.HBM), vmem, vmem],
        out_specs=[vmem] * 3,
        scratch_shapes=[pltpu.SemaphoreType.DMA((layers,))],
        compiler_params=params(12),
        name="fetch",
    )(pltpu.with_memory_space_constraint(weights, pltpu.HBM), *in_vmem(high, low))


def code_blocks(code_ref, parts):
    for j, part in enumerate(parts):
        rows = part.shape[0]
        row = j * (rows + 16)
        code_ref[row : row + rows], code_ref[row + rows : row + rows + 16] = encode(part)


def blocks_of(code_ref):
    rows = code_ref.shape[0] // 2 - 16
    return [decode(code_ref[j * (rows + 16) : j * (rows + 16) + rows], code_ref[j * (rows + 16) + rows : (j + 1) * (rows + 16)]) for j in range(2)]


def rows_of(grads_ref, layer, block, rows):
    return grads_ref[0, layer, pl.ds(pl.multiple_of(block * rows, rows), rows)]


def exact_dot(a, b, dims=PLAIN):
    dot = lambda p, q: lax.dot_general(p, q, (dims, ((), ())), preferred_element_type=jnp.float32)
    return dot(a[0], b) + dot(a[1], b) if isinstance(a, tuple) else dot(a, b[0]) + dot(a, b[1])


def give_kernel(grads_hbm, basis_hbm, code_ref, blocks, basis_ref, sems):
    place = Place()
    layer, rows = place.layer(0), blocks.shape[1]
    copies = [pltpu.make_async_copy(basis_hbm.at[layer], basis_ref, sems.at[2])]
    for j in range(2):
        source = grads_hbm.at[0, layer, pl.ds(pl.multiple_of(place.gives(j) * rows, rows), rows)]
        copies.append(pltpu.make_async_copy(source, blocks.at[j], sems.at[j]))
    for copy in copies:
        copy.start()
    copies[0].wait()
    basis = split(basis_ref[...])
    parts = []
    for j in range(2):
        copies[1 + j].wait()
        parts.append(exact_dot(blocks[j], basis))
    code_blocks(code_ref, parts)


def give(grads, basis):
    rows, (_, width, rank) = grads.shape[2] // 4, basis.shape
    vmem, hbm = pl.BlockSpec(memory_space=pltpu.VMEM), pl.BlockSpec(memory_space=pltpu.HBM)
    return pl.pallas_call(
        give_kernel,
        out_shape=pltpu.VMEM((2 * (rows + 16), rank), jnp.bfloat16),
        in_specs=[hbm, hbm],
        out_specs=vmem,
        scratch_shapes=[
            pltpu.VMEM((2, rows, width), grads.dtype),
            pltpu.VMEM((width, rank), jnp.float32),
            pltpu.SemaphoreType.DMA((3,)),
        ],
        compiler_params=params(8),
        name="give",
    )(*[pltpu.with_memory_space_constraint(x, pltpu.HBM) for x in (grads, basis)])


def project_kernel(turn, grads_ref, high_ref, low_ref, out_ref, *code_refs):
    place = Place()
    layer, rows = place.layer(turn), out_ref.shape[0] // 2
    basis = high_ref[layer], low_ref[layer]
    for code_ref in code_refs:
        code_blocks(code_ref, [exact_dot(rows_of(grads_ref, layer, place.gives(j), rows), basis) for j in range(2)])
    for j in range(2):
        out_ref[j * rows : (j + 1) * rows] = exact_dot(rows_of(grads_ref, layer, place.keeps(j), rows), basis)


def project(grads, basis, turn):
    rows, rank = grads.shape[2] // 4, basis[0].shape[2]
    outs = [((2 * rows, rank), jnp.float32)] + [((2 * (rows + 16), rank), jnp.bfloat16)] * turn
    return local_call(functools.partial(project_kernel, turn), outs, grads, *basis, name="project")


def add_coded_kernel(own_ref, received_ref, out_ref, code_ref):
    rows = own_ref.shape[0] // 2
    parts = [own_ref[j * rows : (j + 1) * rows] + block for j, block in enumerate(blocks_of(received_ref))]
    code_blocks(code_ref, parts)
    for j, part in enumerate(parts):
        out_ref[j * rows : (j + 1) * rows] = part


def add_coded(own, received):
    outs = [(own.shape, jnp.float32), (received.shape, jnp.bfloat16)]
    return local_call(add_coded_kernel, outs, own, received, name="add_coded")


HALVES = 2


def power_kernel(turn, scale, grads_ref, first_ref, second_ref, kept_ref, given_ref, *rest):
    place = Place()
    code_before = rest[2] if turn else None
    half0_ref, half1_ref, one_ref, two_ref, code_ref, product, one, two, sems = rest[3 * turn :]
    rows = first_ref.shape[1]
    sums = [kept_ref[0:rows], kept_ref[rows:]]
    layer = place.layer(turn)
    reduced = scale * jnp.where(place.z < 2, sums[0], sums[1])
    one[...], two[...], direction = adam_direction(reduced, first_ref[layer], second_ref[layer])
    copies = [pltpu.make_async_copy(x, out.at[layer], sems.at[i]) for i, (x, out) in enumerate(((one, one_ref), (two, two_ref)))]
    for copy in copies:
        copy.start()
    if turn == 0:
        code_ref[0:rows], code_ref[rows:] = encode(direction)
    else:
        code_ref[1 - layer] = code_before[...]
        code_ref[layer, 0:rows], code_ref[layer, rows:] = encode(direction)
    blocks = [place.keeps(0), place.keeps(1), place.gives(0), place.gives(1)]
    rows_in_order = jnp.concatenate([rows_of(grads_ref, layer, block, rows) for block in blocks])
    product[...] = exact_dot(split(jnp.concatenate(sums + blocks_of(given_ref)).T), rows_in_order)
    piece = product.shape[0] // (4 * HALVES)
    for h in range(HALVES):
        for k in range(4):
            (half0_ref, half1_ref)[h][pl.ds(k * piece, piece)] = product[pl.ds(place.piece(h, k, piece), piece)]
    for copy in copies:
        copy.wait()


def power_product(grads, first_moment, second_moment, kept, given, turn, scale, before=()):
    width = grads.shape[3]
    layers, rows, rank = first_moment.shape
    vmem, anywhere = pl.BlockSpec(memory_space=pltpu.VMEM), pl.BlockSpec(memory_space=pl.ANY)
    operands = in_vmem(grads, first_moment, second_moment, kept, given)
    count = len(operands)
    return pl.pallas_call(
        functools.partial(power_kernel, turn, scale),
        out_shape=[pltpu.VMEM((rank // HALVES, width), jnp.float32)] * HALVES
        + [jax.ShapeDtypeStruct(first_moment.shape, jnp.float32)] * 2
        + [pltpu.VMEM((layers, rows + 16, rank) if turn else (rows + 16, rank), jnp.bfloat16)],
        in_specs=[vmem] * count + [anywhere, anywhere, vmem][: len(before)],
        out_specs=[vmem] * HALVES + [anywhere] * 2 + [vmem],
        scratch_shapes=[pltpu.VMEM((rank, width), jnp.float32)]
        + [pltpu.VMEM((rows, rank), jnp.float32)] * 2
        + [pltpu.SemaphoreType.DMA((2,))],
        input_output_aliases={count: HALVES, count + 1: HALVES + 1} if before else {},
        compiler_params=params(12),
        cost_estimate=cost(2e9 * turn),
        name="power",
    )(*operands, *before[:2], *in_vmem(*before[2:]))


def add_split_kernel(own_ref, received_ref, keep_ref, give_ref):
    half = keep_ref.shape[0]
    keep_ref[...] = own_ref[0:half] + received_ref[0:half]
    give_ref[...] = own_ref[half:] + received_ref[half:]


def add_split(own, received, flops):
    outs = [((own.shape[0] // 2, own.shape[1]), jnp.float32)] * 2
    return local_call(add_split_kernel, outs, own, received, name="add_split", flops=flops)


def add_kernel(own_ref, received_ref, out_ref):
    out_ref[...] = own_ref[...] + received_ref[...]


def join_kernel(own_ref, received_ref, out_ref):
    half = own_ref.shape[0]
    out_ref[0:half] = own_ref[...]
    out_ref[half:] = received_ref[...]


def add(own, received, flops):
    return local_call(add_kernel, [(own.shape, jnp.float32)], own, received, name="add", flops=flops)[0]


def join(own, received):
    outs = [((2 * own.shape[0], own.shape[1]), jnp.float32)]
    return local_call(join_kernel, outs, own, received, name="join")[0]


def newton_schulz_kernel(*refs):
    place = Place()
    parts, (result_ref, power_ref) = refs[:-2], refs[-2:]
    piece = parts[0].shape[0] // 2
    for h in range(HALVES):
        for k in range(4):
            part = parts[2 * h + k // 2]
            power_ref[pl.ds(place.piece(h, k, piece), piece)] = part[pl.ds(k % 2 * piece, piece)]
    power = power_ref[...]
    rank, width = power.shape
    unscaled = split(power)
    scale = 1.0 / (jnp.sqrt(jnp.sum(power * power)) + norm_eps)
    gram = dot3(unscaled, unscaled, BOTH_LAST) * scale * scale
    ident = lax.broadcasted_iota(jnp.int32, gram.shape, 0) == lax.broadcasted_iota(jnp.int32, gram.shape, 1)
    diagonal = jnp.where(ident, coeff_a, 0.0)
    product = None
    for sweep in range(NS_ITERS - 1):
        g = split(gram)
        factor = diagonal + coeff_b * gram + coeff_c * dot3(g, g)
        f = split(factor)
        gram = dot3(split(dot3(f, g)), f)
        product = f if product is None else split(dot3(product, f))
    iterate = split(dot3(product, unscaled))
    g = split(gram)
    last = split((diagonal + coeff_b * gram + coeff_c * dot3(g, g)) * (scale * width**0.5))
    for i in range(width // rank):
        columns = slice(i * rank, (i + 1) * rank)
        result_ref[columns] = dot3(last, [term[:, columns] for term in iterate]).T


def newton_schulz_power(*parts):
    rank, width = 2 * HALVES * parts[0].shape[0], parts[0].shape[1]
    scratch = [pltpu.VMEM((rank, width), jnp.float32)]
    return local_call(newton_schulz_kernel, [((width, rank), jnp.float32)], *parts, name="newton_schulz", scratch=scratch)[0]


def put_layer_kernel(layer_ref, whole_ref, out_ref, sems):
    count = sems.shape[0]
    rows = layer_ref.shape[0] // count
    copies = []
    for i in range(count):
        part = pl.ds(i * rows, rows)
        copies.append(pltpu.make_async_copy(layer_ref.at[part], out_ref.at[1 - Place().core, part], sems.at[i]))
    for copy in copies:
        copy.start()
    for copy in copies:
        copy.wait()


def put_layer(layer, whole):
    hbm = pl.BlockSpec(memory_space=pl.ANY)
    return pl.pallas_call(
        put_layer_kernel,
        out_shape=jax.ShapeDtypeStruct(whole.shape, whole.dtype),
        in_specs=[pl.BlockSpec(memory_space=pltpu.VMEM), hbm],
        out_specs=hbm,
        scratch_shapes=[pltpu.SemaphoreType.DMA((4,))],
        input_output_aliases={1: 0},
        compiler_params=params(4),
        name="put_layer",
    )(*in_vmem(layer), whole)


def stack_kernel(a_ref, b_ref, out_ref):
    out_ref[0] = a_ref[...]
    out_ref[1] = b_ref[...]


def stack(a, b):
    return local_call(stack_kernel, [((2,) + a.shape, a.dtype)], a, b, name="stack")[0]


def update_kernel(factor, blocks, weights_ref, high_ref, low_ref, *refs):
    directions, (buffer, sems) = refs[:2], refs[-2:]
    place = Place()
    layers, rows = weights_ref.shape[0], buffer.shape[2]
    copies = []
    if len(refs) == 5:
        out_ref = refs[2]
    else:
        own_ref, _, out_ref, basis_ref = refs[2:6]
        copies.append(pltpu.make_async_copy(own_ref, basis_ref.at[place.core], sems.at[layers, 0]))
        copies[0].start()
    for layer in range(layers):
        basis = high_ref[layer], low_ref[layer]
        exact = jnp.concatenate(
            [decode(x[source, layer, 0:rows], x[source, layer, rows:]) for x, (_, source) in zip(directions, blocks)]
        )
        update = dot3(split(exact), basis)
        for i, (k, _) in enumerate(blocks):
            where = pl.ds(pl.multiple_of((place.z ^ k) * rows, rows), rows)
            part = update[i * rows : (i + 1) * rows]
            buffer[layer, i] = (weights_ref[layer, where].astype(jnp.float32) - factor * part).astype(buffer.dtype)
            copies.append(pltpu.make_async_copy(buffer.at[layer, i], out_ref.at[layer, where], sems.at[layer, i]))
            copies[-1].start()
    for copy in copies:
        copy.wait()


def update_weights(weights, basis, directions, blocks, factor, flops, own=None, before=None):
    layers, height, width = weights.shape
    vmem, anywhere = pl.BlockSpec(memory_space=pltpu.VMEM), pl.BlockSpec(memory_space=pl.ANY)
    last = before is not None
    operands = in_vmem(weights, *basis, *directions, *([own] if last else []))
    outs = [jax.ShapeDtypeStruct(weights.shape, weights.dtype)]
    if last:
        outs.append(jax.ShapeDtypeStruct((layers,) + own.shape, own.dtype))
    return pl.pallas_call(
        functools.partial(update_kernel, factor, blocks),
        out_shape=outs,
        in_specs=[vmem] * len(operands) + [anywhere] * last,
        out_specs=[anywhere] * len(outs),
        scratch_shapes=[pltpu.VMEM((layers, 2, height // 4, width), weights.dtype), pltpu.SemaphoreType.DMA((layers + 1, 2))],
        input_output_aliases={6: 0} if last else {},
        compiler_params=params(12),
        cost_estimate=cost(flops),
        name="update_weights",
    )(*operands, *([before] if last else []))


def xor_pairs(k):
    return [(i, i ^ k) for i in range(4)]


def over_z(x, k):
    return lax.ppermute(x, "shard", xor_pairs(k))


def over_core(x):
    return lax.ppermute(x, "tensor", xor_pairs(1))


def over_y(x):
    return lax.ppermute(x, "tensor", xor_pairs(2))


class Order:
    def __init__(self):
        self.last = None

    def step(self, *operands):
        if self.last is None:
            return operands
        return lax.optimization_barrier(tuple(operands) + (self.last,))[:-1]

    def through(self, result):
        self.last = result
        return result


def line_body(grads, weights, basis, first_moment, second_moment):
    width = basis.shape[1]
    scale_factor = width ** (-0.5)
    layers, rows = grads.shape[1], first_moment.shape[1]
    order = Order()


    def product(turn, kept, given, *before):
        *halves, one, two, code = power_product(
            grads, first_moment, second_moment, *order.step(kept, given), turn, scale_factor, before
        )
        order.through(halves[0])
        return halves, (one, two, code)

    def add_code(x, received):
        x, code = add_coded(*order.step(x, received))
        return order.through(x), code

    def scatter(over, x, received, flops=0):
        keep, give = add_split(*order.step(x, received), flops)
        return order.through(keep), over(give)

    def total(over, x, received, flops=0):
        x = order.through(add(*order.step(x, received), flops))
        return x, over(x)

    def gather(over, x, received):
        x = order.through(join(*order.step(x, received)))
        return x, over(x)

    next_z = lambda x: over_z(x, 1)
    opposite_z = lambda x: over_z(x, 3)

    code = order.through(give(grads, basis))
    received = next_z(code)
    grads, high, low = prepare(*order.step(grads, basis))
    (kept,) = project(grads, (high, low), 0)
    second, second_code = project(*order.step(grads, order.through(kept))[:1], (high, low), 1)
    order.through(second)
    weights, *turned = fetch(*order.step(weights, high, low))
    order.through(weights)
    first, code = add_code(kept, received)
    first = first, opposite_z(code)
    second, code = add_code(second, next_z(order.step(second_code)[0]))
    second = second, opposite_z(code)
    sums = []
    for pair in (first, second):
        x, code = add_code(*pair)
        sums.append((x, next_z(code)))
    gifts, before = product(0, *sums[0])
    gifts = [over_core(gift) for gift in gifts]
    parts, (moment_one, moment_two, code) = product(1, *sums[1], *before)
    parts = [scatter(over_y, part, gift, 1e9) for part, gift in zip(parts, gifts)]
    opposite = opposite_z(order.step(code)[0])
    parts = [scatter(next_z, *part) for part in parts]
    opposite, *parts[0] = order.step(opposite, *parts[0])
    first = total(opposite_z, *parts[0], 1e9)
    parts = [first, total(opposite_z, *parts[1])]
    parts = [total(next_z, *part) for part in parts]
    parts = [gather(over_y, *part) for part in parts]
    pair = next_z(order.through(stack(*order.step(code, opposite))))
    factor = learn_rate * galore_scale * scale_factor
    code, opposite, weights, *parts[0] = order.step(code[None], opposite[None], weights, *parts[0])
    (weights_next,) = update_weights(weights, turned, (code, opposite), ((0, 0), (3, 0)), factor, 3e9)
    order.through(weights_next)
    parts = order.step(*[x for part in parts for x in part])
    own = newton_schulz_power(*parts)
    order.through(own)
    other = over_core(own)
    (pair,) = order.step(pair)
    weights_next, basis_next = update_weights(weights, turned, (pair, pair), ((1, 0), (2, 1)), factor, 8e9, own, weights_next)
    order.through(weights_next)
    basis_next = put_layer(*order.step(other, basis_next))
    return (weights_next, basis_next, moment_one, moment_two)


def solution(mesh):
    line = mesh.shape["shard"] == 4 and mesh.shape["tensor"] == 4

    def body(grads, *others):
        return (line_body if line and grads.shape[1] == 2 else general_body)(grads, *others)

    return jax.shard_map(
        body,
        mesh=mesh,
        in_specs=(
            P("shard", "section", "tensor", None),
            P("section", "tensor", None),
            P("section", None, None),
            P("section", ("tensor", "shard"), None),
            P("section", ("tensor", "shard"), None),
        ),
        out_specs=(
            P("section", "tensor", None),
            P("section", None, None),
            P("section", ("tensor", "shard"), None),
            P("section", ("tensor", "shard"), None),
        ),
        check_vma=False,
    )
```

```python
import functools

import jax
import jax.numpy as jnp
from jax import lax
from jax.experimental import pallas as pl
from jax.experimental.pallas import tpu as pltpu
from jax.sharding import PartitionSpec as P

NS_ITERS = 3
STEP = 1000


learn_rate = 0.5
galore_scale = 0.25
beta_one = 0.9
beta_two = 0.999
adam_eps = 1e-08
norm_eps = 1e-07
coeff_a = 3.4445
coeff_b = -4.775
coeff_c = 2.0315
highest = lax.Precision.HIGHEST


def newton_step(iterate, gram_matrix):
    squared = jnp.einsum("lrs,lst->lrt", gram_matrix, gram_matrix, precision=highest)
    mixing = coeff_b * gram_matrix + coeff_c * squared
    return coeff_a * iterate + jnp.einsum("ldr,lrs->lds", iterate, mixing, precision=highest)


def adam_direction(reduced, first_moment, second_moment):
    moment_one = beta_one * first_moment + (1.0 - beta_one) * reduced
    moment_two = beta_two * second_moment + (1.0 - beta_two) * reduced * reduced
    corrected_one = moment_one / (1.0 - beta_one**STEP)
    corrected_two = moment_two / (1.0 - beta_two**STEP)
    return (moment_one, moment_two, corrected_one / (jnp.sqrt(corrected_two) + adam_eps))


def newton_schulz(power, width):
    norms = jnp.sqrt(jnp.sum(power * power, axis=(1, 2)))
    iterate = power / (norms + norm_eps)[:, None, None]
    for sweep in range(NS_ITERS):
        gram_matrix = jnp.einsum("ldr,lds->lrs", iterate, iterate, precision=highest)
        iterate = newton_step(iterate, gram_matrix)
    return width**0.5 * iterate


def general_body(grads, weights, basis, first_moment, second_moment):
    width = basis.shape[1]
    scale_factor = width ** (-0.5)
    local_grads = grads[0]
    block_rows = first_moment.shape[1]
    summed = lax.psum_scatter(
        local_grads.astype(jnp.float32), "shard", scatter_dimension=1, tiled=True
    )
    projected = jnp.einsum("lfd,ldr->lfr", summed, basis, precision=highest)
    power = jnp.einsum("lfd,lfr->ldr", summed, projected, precision=highest)
    reduced = scale_factor * projected
    moment_one, moment_two, direction = adam_direction(reduced, first_moment, second_moment)
    factor = learn_rate * galore_scale * scale_factor
    own_start = lax.axis_index("shard") * block_rows
    current = lax.dynamic_slice_in_dim(weights, own_start, block_rows, 1)
    update = jnp.einsum("lfr,ldr->lfd", direction, basis, precision=highest)
    fresh_rows = (current.astype(jnp.float32) - factor * update).astype(jnp.bfloat16)
    weights_next = lax.all_gather(fresh_rows, "shard", axis=1, tiled=True)
    whole = lax.psum(power, ("shard", "tensor"))
    basis_next = newton_schulz(whole, width)
    return (weights_next, basis_next, moment_one, moment_two)


PLAIN = ((1,), (0,))
BOTH_LAST = ((1,), (1,))


class Place:
    def __init__(self):
        tensor, self.z = lax.axis_index("tensor"), lax.axis_index("shard")
        self.core, self.y = lax.rem(tensor, 2), lax.div(tensor, 2)
        self.inner = lax.div(lax.rem(self.z + 1, 4), 2)

    def keeps(self, j):
        return jnp.where(self.inner == 1, 1 + j, 3 * j)

    def gives(self, j):
        return jnp.where(self.inner == 1, 3 * j, 1 + j)

    def layer(self, turn):
        return self.core if turn else 1 - self.core

    def piece(self, h, k, piece):
        return pl.multiple_of((h * 4 + (self.y ^ (k // 2)) * 2 + (self.inner ^ (k % 2))) * piece, piece)


def split(x):
    high = x.astype(jnp.bfloat16)
    return high, (x - high.astype(jnp.float32)).astype(jnp.bfloat16)


def dot3(a, b, dims=PLAIN):
    dot = lambda p, q: lax.dot_general(p, q, (dims, ((), ())), preferred_element_type=jnp.float32)
    return dot(a[0], b[0]) + (dot(a[0], b[1]) + dot(a[1], b[0]))


def params(megabytes):
    return pltpu.CompilerParams(vmem_limit_bytes=megabytes * 2**20)


def in_vmem(*arrays):
    return [pltpu.with_memory_space_constraint(x, pltpu.VMEM) for x in arrays]


def local_call(kernel, outs, *operands, name, scratch=(), flops=0):
    vmem = pl.BlockSpec(memory_space=pltpu.VMEM)
    return pl.pallas_call(
        kernel,
        out_shape=[pltpu.VMEM(shape, dtype) for shape, dtype in outs],
        in_specs=[vmem] * len(operands),
        out_specs=[vmem] * len(outs),
        scratch_shapes=scratch,
        compiler_params=params(12),
        cost_estimate=cost(flops),
        name=name,
    )(*in_vmem(*operands))


def cost(flops):
    return pl.CostEstimate(flops=int(flops), bytes_accessed=0, transcendentals=0) if flops else None


SPAN = 250.0


def encode(x):
    bound = jnp.max(jnp.abs(x), axis=0, keepdims=True)
    bound = (bound * 1.01 + 1e-30).astype(jnp.bfloat16).astype(jnp.float32)
    size = jnp.exp2(jnp.abs(x) * (SPAN / bound) - SPAN / 2)
    code = jnp.where(x < 0, -size, size)
    return code.astype(jnp.bfloat16), jnp.broadcast_to(bound, (16, x.shape[1])).astype(jnp.bfloat16)


def decode(code, bound):
    code, bound = code.astype(jnp.float32), bound[0:1].astype(jnp.float32)
    size = (jnp.log2(jnp.abs(code)) + SPAN / 2) * (bound / SPAN)
    return jnp.where(code < 0, -size, size)


def prepare_kernel(grads_hbm, basis_hbm, grads_ref, high_ref, low_ref, buffer, sems):
    layers = buffer.shape[0]
    copies = [pltpu.make_async_copy(basis_hbm.at[layer], buffer.at[layer], sems.at[layer]) for layer in range(layers)]
    copies += [pltpu.make_async_copy(grads_hbm.at[0, layer], grads_ref.at[0, layer], sems.at[layers + layer]) for layer in range(layers)]
    for copy in copies:
        copy.start()
    for layer in range(layers):
        copies[layer].wait()
        high_ref[layer], low_ref[layer] = split(buffer[layer])
    for copy in copies[layers:]:
        copy.wait()


def prepare(grads, basis):
    layers = basis.shape[0]
    vmem, hbm = pl.BlockSpec(memory_space=pltpu.VMEM), pl.BlockSpec(memory_space=pltpu.HBM)
    return pl.pallas_call(
        prepare_kernel,
        out_shape=[pltpu.VMEM(grads.shape, grads.dtype)] + [pltpu.VMEM(basis.shape, jnp.bfloat16)] * 2,
        in_specs=[hbm, hbm],
        out_specs=[vmem] * 3,
        scratch_shapes=[pltpu.VMEM(basis.shape, jnp.float32), pltpu.SemaphoreType.DMA((2 * layers,))],
        compiler_params=params(12),
        name="prepare",
    )(*[pltpu.with_memory_space_constraint(x, pltpu.HBM) for x in (grads, basis)])


def fetch_kernel(weights_hbm, high_ref, low_ref, weights_ref, high_t_ref, low_t_ref, sems):
    layers = weights_ref.shape[0]
    copies = [pltpu.make_async_copy(weights_hbm.at[layer], weights_ref.at[layer], sems.at[layer]) for layer in range(layers)]
    for copy in copies:
        copy.start()
    for layer in range(layers):
        for source, out in ((high_ref, high_t_ref), (low_ref, low_t_ref)):
            out[layer] = source[layer].astype(jnp.float32).T.astype(jnp.bfloat16)
    for copy in copies:
        copy.wait()


def fetch(weights, high, low):
    layers, width, rank = high.shape
    vmem = pl.BlockSpec(memory_space=pltpu.VMEM)
    return pl.pallas_call(
        fetch_kernel,
        out_shape=[pltpu.VMEM(weights.shape, weights.dtype)] + [pltpu.VMEM((layers, rank, width), jnp.bfloat16)] * 2,
        in_specs=[pl.BlockSpec(memory_space=pltpu.HBM), vmem, vmem],
        out_specs=[vmem] * 3,
        scratch_shapes=[pltpu.SemaphoreType.DMA((layers,))],
        compiler_params=params(12),
        name="fetch",
    )(pltpu.with_memory_space_constraint(weights, pltpu.HBM), *in_vmem(high, low))


def code_blocks(code_ref, parts):
    for j, part in enumerate(parts):
        rows = part.shape[0]
        row = j * (rows + 16)
        code_ref[row : row + rows], code_ref[row + rows : row + rows + 16] = encode(part)


def blocks_of(code_ref):
    rows = code_ref.shape[0] // 2 - 16
    return [decode(code_ref[j * (rows + 16) : j * (rows + 16) + rows], code_ref[j * (rows + 16) + rows : (j + 1) * (rows + 16)]) for j in range(2)]


def rows_of(grads_ref, layer, block, rows):
    return grads_ref[0, layer, pl.ds(pl.multiple_of(block * rows, rows), rows)]


def exact_dot(a, b, dims=PLAIN):
    dot = lambda p, q: lax.dot_general(p, q, (dims, ((), ())), preferred_element_type=jnp.float32)
    return dot(a[0], b) + dot(a[1], b) if isinstance(a, tuple) else dot(a, b[0]) + dot(a, b[1])


def give_kernel(grads_hbm, basis_hbm, code_ref, blocks, basis_ref, sems):
    place = Place()
    layer, rows = place.layer(0), blocks.shape[1]
    copies = [pltpu.make_async_copy(basis_hbm.at[layer], basis_ref, sems.at[2])]
    for j in range(2):
        source = grads_hbm.at[0, layer, pl.ds(pl.multiple_of(place.gives(j) * rows, rows), rows)]
        copies.append(pltpu.make_async_copy(source, blocks.at[j], sems.at[j]))
    for copy in copies:
        copy.start()
    copies[0].wait()
    basis = split(basis_ref[...])
    parts = []
    for j in range(2):
        copies[1 + j].wait()
        parts.append(exact_dot(blocks[j], basis))
    code_blocks(code_ref, parts)


def give(grads, basis):
    rows, (_, width, rank) = grads.shape[2] // 4, basis.shape
    vmem, hbm = pl.BlockSpec(memory_space=pltpu.VMEM), pl.BlockSpec(memory_space=pltpu.HBM)
    return pl.pallas_call(
        give_kernel,
        out_shape=pltpu.VMEM((2 * (rows + 16), rank), jnp.bfloat16),
        in_specs=[hbm, hbm],
        out_specs=vmem,
        scratch_shapes=[
            pltpu.VMEM((2, rows, width), grads.dtype),
            pltpu.VMEM((width, rank), jnp.float32),
            pltpu.SemaphoreType.DMA((3,)),
        ],
        compiler_params=params(8),
        name="give",
    )(*[pltpu.with_memory_space_constraint(x, pltpu.HBM) for x in (grads, basis)])


def project_kernel(turn, grads_ref, high_ref, low_ref, out_ref, *code_refs):
    place = Place()
    layer, rows = place.layer(turn), out_ref.shape[0] // 2
    basis = high_ref[layer], low_ref[layer]
    for code_ref in code_refs:
        code_blocks(code_ref, [exact_dot(rows_of(grads_ref, layer, place.gives(j), rows), basis) for j in range(2)])
    for j in range(2):
        out_ref[j * rows : (j + 1) * rows] = exact_dot(rows_of(grads_ref, layer, place.keeps(j), rows), basis)


def project(grads, basis, turn):
    rows, rank = grads.shape[2] // 4, basis[0].shape[2]
    outs = [((2 * rows, rank), jnp.float32)] + [((2 * (rows + 16), rank), jnp.bfloat16)] * turn
    return local_call(functools.partial(project_kernel, turn), outs, grads, *basis, name="project")


def add_coded_kernel(own_ref, received_ref, out_ref, code_ref):
    rows = own_ref.shape[0] // 2
    parts = [own_ref[j * rows : (j + 1) * rows] + block for j, block in enumerate(blocks_of(received_ref))]
    code_blocks(code_ref, parts)
    for j, part in enumerate(parts):
        out_ref[j * rows : (j + 1) * rows] = part


def add_coded(own, received):
    outs = [(own.shape, jnp.float32), (received.shape, jnp.bfloat16)]
    return local_call(add_coded_kernel, outs, own, received, name="add_coded")


HALVES = 2


def power_kernel(turn, scale, grads_ref, first_ref, second_ref, kept_ref, given_ref, *rest):
    place = Place()
    code_before = rest[2] if turn else None
    half0_ref, half1_ref, one_ref, two_ref, code_ref, product, one, two, sems = rest[3 * turn :]
    rows = first_ref.shape[1]
    sums = [kept_ref[0:rows], kept_ref[rows:]]
    layer = place.layer(turn)
    reduced = scale * jnp.where(place.z < 2, sums[0], sums[1])
    one[...], two[...], direction = adam_direction(reduced, first_ref[layer], second_ref[layer])
    copies = [pltpu.make_async_copy(x, out.at[layer], sems.at[i]) for i, (x, out) in enumerate(((one, one_ref), (two, two_ref)))]
    for copy in copies:
        copy.start()
    if turn == 0:
        code_ref[0:rows], code_ref[rows:] = encode(direction)
    else:
        code_ref[1 - layer] = code_before[...]
        code_ref[layer, 0:rows], code_ref[layer, rows:] = encode(direction)
    blocks = [place.keeps(0), place.keeps(1), place.gives(0), place.gives(1)]
    rows_in_order = jnp.concatenate([rows_of(grads_ref, layer, block, rows) for block in blocks])
    product[...] = exact_dot(split(jnp.concatenate(sums + blocks_of(given_ref)).T), rows_in_order)
    piece = product.shape[0] // (4 * HALVES)
    for h in range(HALVES):
        for k in range(4):
            (half0_ref, half1_ref)[h][pl.ds(k * piece, piece)] = product[pl.ds(place.piece(h, k, piece), piece)]
    for copy in copies:
        copy.wait()


def power_product(grads, first_moment, second_moment, kept, given, turn, scale, before=()):
    width = grads.shape[3]
    layers, rows, rank = first_moment.shape
    vmem, anywhere = pl.BlockSpec(memory_space=pltpu.VMEM), pl.BlockSpec(memory_space=pl.ANY)
    operands = in_vmem(grads, first_moment, second_moment, kept, given)
    count = len(operands)
    return pl.pallas_call(
        functools.partial(power_kernel, turn, scale),
        out_shape=[pltpu.VMEM((rank // HALVES, width), jnp.float32)] * HALVES
        + [jax.ShapeDtypeStruct(first_moment.shape, jnp.float32)] * 2
        + [pltpu.VMEM((layers, rows + 16, rank) if turn else (rows + 16, rank), jnp.bfloat16)],
        in_specs=[vmem] * count + [anywhere, anywhere, vmem][: len(before)],
        out_specs=[vmem] * HALVES + [anywhere] * 2 + [vmem],
        scratch_shapes=[pltpu.VMEM((rank, width), jnp.float32)]
        + [pltpu.VMEM((rows, rank), jnp.float32)] * 2
        + [pltpu.SemaphoreType.DMA((2,))],
        input_output_aliases={count: HALVES, count + 1: HALVES + 1} if before else {},
        compiler_params=params(12),
        cost_estimate=cost(2e9 * turn),
        name="power",
    )(*operands, *before[:2], *in_vmem(*before[2:]))


def add_split_kernel(own_ref, received_ref, keep_ref, give_ref):
    half = keep_ref.shape[0]
    keep_ref[...] = own_ref[0:half] + received_ref[0:half]
    give_ref[...] = own_ref[half:] + received_ref[half:]


def add_split(own, received, flops):
    outs = [((own.shape[0] // 2, own.shape[1]), jnp.float32)] * 2
    return local_call(add_split_kernel, outs, own, received, name="add_split", flops=flops)


def add_kernel(own_ref, received_ref, out_ref):
    out_ref[...] = own_ref[...] + received_ref[...]


def join_kernel(own_ref, received_ref, out_ref):
    half = own_ref.shape[0]
    out_ref[0:half] = own_ref[...]
    out_ref[half:] = received_ref[...]


def add(own, received, flops):
    return local_call(add_kernel, [(own.shape, jnp.float32)], own, received, name="add", flops=flops)[0]


def join(own, received):
    outs = [((2 * own.shape[0], own.shape[1]), jnp.float32)]
    return local_call(join_kernel, outs, own, received, name="join")[0]


def newton_schulz_kernel(*refs):
    place = Place()
    parts, (result_ref, power_ref) = refs[:-2], refs[-2:]
    piece = parts[0].shape[0] // 2
    for h in range(HALVES):
        for k in range(4):
            part = parts[2 * h + k // 2]
            power_ref[pl.ds(place.piece(h, k, piece), piece)] = part[pl.ds(k % 2 * piece, piece)]
    power = power_ref[...]
    rank, width = power.shape
    unscaled = split(power)
    scale = 1.0 / (jnp.sqrt(jnp.sum(power * power)) + norm_eps)
    gram = dot3(unscaled, unscaled, BOTH_LAST) * scale * scale
    ident = lax.broadcasted_iota(jnp.int32, gram.shape, 0) == lax.broadcasted_iota(jnp.int32, gram.shape, 1)
    diagonal = jnp.where(ident, coeff_a, 0.0)
    product = None
    for sweep in range(NS_ITERS - 1):
        g = split(gram)
        factor = diagonal + coeff_b * gram + coeff_c * dot3(g, g)
        f = split(factor)
        gram = dot3(split(dot3(f, g)), f)
        product = f if product is None else split(dot3(product, f))
    iterate = split(dot3(product, unscaled))
    g = split(gram)
    last = split((diagonal + coeff_b * gram + coeff_c * dot3(g, g)) * (scale * width**0.5))
    result_ref[...] = dot3(last, iterate).T


def newton_schulz_power(*parts):
    rank, width = 2 * HALVES * parts[0].shape[0], parts[0].shape[1]
    scratch = [pltpu.VMEM((rank, width), jnp.float32)]
    return local_call(newton_schulz_kernel, [((width, rank), jnp.float32)], *parts, name="newton_schulz", scratch=scratch)[0]


def put_layer_kernel(layer_ref, whole_ref, out_ref, sems):
    count = sems.shape[0]
    rows = layer_ref.shape[0] // count
    copies = []
    for i in range(count):
        part = pl.ds(i * rows, rows)
        copies.append(pltpu.make_async_copy(layer_ref.at[part], out_ref.at[1 - Place().core, part], sems.at[i]))
    for copy in copies:
        copy.start()
    for copy in copies:
        copy.wait()


def put_layer(layer, whole):
    hbm = pl.BlockSpec(memory_space=pl.ANY)
    return pl.pallas_call(
        put_layer_kernel,
        out_shape=jax.ShapeDtypeStruct(whole.shape, whole.dtype),
        in_specs=[pl.BlockSpec(memory_space=pltpu.VMEM), hbm],
        out_specs=hbm,
        scratch_shapes=[pltpu.SemaphoreType.DMA((8,))],
        input_output_aliases={1: 0},
        compiler_params=params(4),
        name="put_layer",
    )(*in_vmem(layer), whole)


def stack_kernel(a_ref, b_ref, out_ref):
    out_ref[0] = a_ref[...]
    out_ref[1] = b_ref[...]


def stack(a, b):
    return local_call(stack_kernel, [((2,) + a.shape, a.dtype)], a, b, name="stack")[0]


def update_kernel(factor, blocks, weights_ref, high_ref, low_ref, *refs):
    directions, (buffer, sems) = refs[:2], refs[-2:]
    place = Place()
    layers, rows = weights_ref.shape[0], buffer.shape[2]
    copies = []
    if len(refs) == 5:
        out_ref = refs[2]
    else:
        own_ref, _, out_ref, basis_ref = refs[2:6]
        copies.append(pltpu.make_async_copy(own_ref, basis_ref.at[place.core], sems.at[layers, 0]))
        copies[0].start()
    for layer in range(layers):
        basis = high_ref[layer], low_ref[layer]
        exact = jnp.concatenate(
            [decode(x[source, layer, 0:rows], x[source, layer, rows:]) for x, (_, source) in zip(directions, blocks)]
        )
        update = dot3(split(exact), basis)
        for i, (k, _) in enumerate(blocks):
            where = pl.ds(pl.multiple_of((place.z ^ k) * rows, rows), rows)
            part = update[i * rows : (i + 1) * rows]
            buffer[layer, i] = (weights_ref[layer, where].astype(jnp.float32) - factor * part).astype(buffer.dtype)
            copies.append(pltpu.make_async_copy(buffer.at[layer, i], out_ref.at[layer, where], sems.at[layer, i]))
            copies[-1].start()
    for copy in copies:
        copy.wait()


def update_weights(weights, basis, directions, blocks, factor, flops, own=None, before=None):
    layers, height, width = weights.shape
    vmem, anywhere = pl.BlockSpec(memory_space=pltpu.VMEM), pl.BlockSpec(memory_space=pl.ANY)
    last = before is not None
    operands = in_vmem(weights, *basis, *directions, *([own] if last else []))
    outs = [jax.ShapeDtypeStruct(weights.shape, weights.dtype)]
    if last:
        outs.append(jax.ShapeDtypeStruct((layers,) + own.shape, own.dtype))
    return pl.pallas_call(
        functools.partial(update_kernel, factor, blocks),
        out_shape=outs,
        in_specs=[vmem] * len(operands) + [anywhere] * last,
        out_specs=[anywhere] * len(outs),
        scratch_shapes=[pltpu.VMEM((layers, 2, height // 4, width), weights.dtype), pltpu.SemaphoreType.DMA((layers + 1, 2))],
        input_output_aliases={6: 0} if last else {},
        compiler_params=params(12),
        cost_estimate=cost(flops),
        name="update_weights",
    )(*operands, *([before] if last else []))


def xor_pairs(k):
    return [(i, i ^ k) for i in range(4)]


def over_z(x, k):
    return lax.ppermute(x, "shard", xor_pairs(k))


def over_core(x):
    return lax.ppermute(x, "tensor", xor_pairs(1))


def over_y(x):
    return lax.ppermute(x, "tensor", xor_pairs(2))


class Order:
    def __init__(self):
        self.last = None

    def step(self, *operands):
        if self.last is None:
            return operands
        return lax.optimization_barrier(tuple(operands) + (self.last,))[:-1]

    def through(self, result):
        self.last = result
        return result


def line_body(grads, weights, basis, first_moment, second_moment):
    width = basis.shape[1]
    scale_factor = width ** (-0.5)
    layers, rows = grads.shape[1], first_moment.shape[1]
    order = Order()


    def product(turn, kept, given, *before):
        *halves, one, two, code = power_product(
            grads, first_moment, second_moment, *order.step(kept, given), turn, scale_factor, before
        )
        order.through(halves[0])
        return halves, (one, two, code)

    def add_code(x, received):
        x, code = add_coded(*order.step(x, received))
        return order.through(x), code

    def scatter(over, x, received, flops=0):
        keep, give = add_split(*order.step(x, received), flops)
        return order.through(keep), over(give)

    def total(over, x, received, flops=0):
        x = order.through(add(*order.step(x, received), flops))
        return x, over(x)

    def gather(over, x, received):
        x = order.through(join(*order.step(x, received)))
        return x, over(x)

    next_z = lambda x: over_z(x, 1)
    opposite_z = lambda x: over_z(x, 3)

    code = order.through(give(grads, basis))
    received = next_z(code)
    grads, high, low = prepare(*order.step(grads, basis))
    (kept,) = project(grads, (high, low), 0)
    second, second_code = project(*order.step(grads, order.through(kept))[:1], (high, low), 1)
    order.through(second)
    weights, *turned = fetch(*order.step(weights, high, low))
    order.through(weights)
    first, code = add_code(kept, received)
    first = first, opposite_z(code)
    second, code = add_code(second, next_z(order.step(second_code)[0]))
    second = second, opposite_z(code)
    sums = []
    for pair in (first, second):
        x, code = add_code(*pair)
        sums.append((x, next_z(code)))
    gifts, before = product(0, *sums[0])
    gifts = [over_core(gift) for gift in gifts]
    parts, (moment_one, moment_two, code) = product(1, *sums[1], *before)
    parts = [scatter(over_y, part, gift, 1e9) for part, gift in zip(parts, gifts)]
    opposite = opposite_z(order.step(code)[0])
    parts = [scatter(next_z, *part) for part in parts]
    opposite, *parts[0] = order.step(opposite, *parts[0])
    first = total(opposite_z, *parts[0], 1e9)
    parts = [first, total(opposite_z, *parts[1])]
    parts = [total(next_z, *part) for part in parts]
    parts = [gather(over_y, *part) for part in parts]
    pair = next_z(order.through(stack(*order.step(code, opposite))))
    factor = learn_rate * galore_scale * scale_factor
    code, opposite, weights, *parts[0] = order.step(code[None], opposite[None], weights, *parts[0])
    (weights_next,) = update_weights(weights, turned, (code, opposite), ((0, 0), (3, 0)), factor, 3e9)
    order.through(weights_next)
    parts = order.step(*[x for part in parts for x in part])
    own = newton_schulz_power(*parts)
    order.through(own)
    other = over_core(own)
    (pair,) = order.step(pair)
    weights_next, basis_next = update_weights(weights, turned, (pair, pair), ((1, 0), (2, 1)), factor, 8e9, own, weights_next)
    order.through(weights_next)
    basis_next = put_layer(*order.step(other, basis_next))
    return (weights_next, basis_next, moment_one, moment_two)


def solution(mesh):
    line = mesh.shape["shard"] == 4 and mesh.shape["tensor"] == 4

    def body(grads, *others):
        return (line_body if line and grads.shape[1] == 2 else general_body)(grads, *others)

    return jax.shard_map(
        body,
        mesh=mesh,
        in_specs=(
            P("shard", "section", "tensor", None),
            P("section", "tensor", None),
            P("section", None, None),
            P("section", ("tensor", "shard"), None),
            P("section", ("tensor", "shard"), None),
        ),
        out_specs=(
            P("section", "tensor", None),
            P("section", None, None),
            P("section", ("tensor", "shard"), None),
            P("section", ("tensor", "shard"), None),
        ),
        check_vma=False,
    )
```
